256 devices in a mesh: group: 32 (over y, z), head: 8 (over x, core).
Axes of the slice: x: 4, y: 4, z: 8, core: 2. Of those that a mesh axis runs over, the one named last changes fastest.
Arguments:
- query_states: bfloat16 [8192, 5120], P('group', 'head'), may hold values from -110 to 110
- key_states: bfloat16 [8192, 5120], P('group', 'head'), may hold values from -5 to 5
- value_states: bfloat16 [8192, 5120], P('group', 'head'), may hold values from -6 to 6
- hidden: bfloat16 [8192, 5120], P('group', 'head'), may hold values from -3 to 3
- out_weight: bfloat16 [5120, 5120], P('head'), may hold values from -0.078125 to 0.078125
- gate_table: float32 [1000, 5120], P(None, 'head'), may hold values from 0.3 to 3
- levels: int32 [64], P('group'), may hold values from 0 to 999
- visible: int32 [64, 64], replicated, may hold values 0 or 1
- incoming: bfloat16 [128, 5120], P(None, 'head'), may hold values from -6 to 6
Outputs:
- queue_next: bfloat16 [8192, 5120], P('group', 'head')
The draws below stay inside these ranges and needn't reach their ends.
All inputs are finite; a program needn't handle non-finite values.
Results may differ from the reference program's by a relative error of at most 0.015.
Values may be sent and summed in bfloat16 or wider, within the bound.
A program may use at most 128 MiB of HBM per device.

```python
import math
import jax
import jax.numpy as jnp
from jax import lax

D = 5120
HEADS = 40
LEVELS = 1000
HD = 128
TOK = 128
GROUPS = 64


def draw_query_states(key, part):
    key = jax.random.fold_in(key, 3)
    shape = (GROUPS * TOK, HEADS * HD)
    result = 2.5 * jnp.clip(jax.random.normal(key, shape, jnp.float32), -4.0, 4.0)
    return result.astype(jnp.bfloat16)


def draw_key_states(key, part):
    key = jax.random.fold_in(key, 5)
    shape = (GROUPS * TOK, HEADS * HD)
    result = jnp.clip(jax.random.normal(key, shape, jnp.float32), -4.0, 4.0)
    return result.astype(jnp.bfloat16)


def place_ends(values, key, low, largest):
    longest = values.shape.index(max(values.shape))
    spots = []
    for shift in (0, 1):
        where = [jax.random.randint(jax.random.fold_in(key, axis), (), 0, length) for axis, length in enumerate(values.shape)]
        where[longest] = (where[longest] + shift) % values.shape[longest]
        spots.append(tuple(where))
    return values.at[spots[0]].set(low).at[spots[1]].set(largest)


def block_scale(rng, shape, split, low, top_value):
    def one(dim, blocks):
        steps = jax.random.uniform(jax.random.fold_in(jax.random.fold_in(rng, 6), dim), (blocks,), jnp.float32, low / len(split), top_value / len(split))
        return jnp.repeat(jnp.exp(steps), shape[dim] // blocks).reshape((-1,) + (1,) * (len(shape) - dim - 1))

    gain = one(*split[0])
    for cut in split[1:]:
        gain = gain * one(*cut)
    return gain


def gaussian(rng, shape, spread, bound, pieces=(), held_as=jnp.bfloat16):
    drawn = spread * jax.random.normal(rng, shape, jnp.float32)
    if pieces:
        drawn = drawn * block_scale(rng, shape, pieces, -0.22, 0.18)
    return jnp.clip(drawn, -bound, bound).astype(held_as)


def setup_inputs(seed: int = 0) -> dict:
    keys = jax.random.split(jax.random.key(seed), 10)
    return {
        "query_states": draw_query_states(jax.random.fold_in(keys[9], 71), 0),
        "key_states": draw_key_states(jax.random.fold_in(keys[9], 71), 0),
        "value_states": gaussian(keys[2], (GROUPS * TOK, HEADS * HD), 1.0, 6.0, ((0, 32), (1, 8))),
        "hidden": gaussian(keys[3], (GROUPS * TOK, D), 0.5, 3.0, ((0, 32), (1, 8))),
        "out_weight": gaussian(keys[4], (HEADS * HD, D), (HEADS * HD) ** -0.5, 0.078125, ((0, 8),)),
        "gate_table": jnp.clip(jnp.exp(math.log(3.0) - 2.3025851 * jax.random.uniform(keys[5], (LEVELS, D), jnp.float32) ** block_scale(keys[5], (LEVELS, D), ((1, 8),), -0.2, 0.2)), 0.3, 3.0),
        "levels": place_ends(jax.random.randint(keys[6], (GROUPS,), 0, LEVELS), jax.random.fold_in(keys[6], 1), 0, LEVELS - 1).astype(jnp.int32),
        "visible": place_ends((jax.random.randint(keys[7], (GROUPS, GROUPS), 0, 4) < 3).astype(jnp.int32), jax.random.fold_in(keys[7], 1), 0, 1),
        "incoming": gaussian(keys[8], (TOK, D), 1.0, 6.0, ((1, 8),)),
    }


def reference(query_states, key_states, value_states, hidden, out_weight, gate_table, levels, visible, incoming):
    query_heads = query_states.reshape(GROUPS, TOK, HEADS, HD)
    key_heads = key_states.reshape(GROUPS * TOK, HEADS, HD)
    value_heads = value_states.reshape(GROUPS * TOK, HEADS, HD)
    key_group = (jnp.arange(GROUPS * TOK) // TOK).astype(jnp.int32)
    scale = 1.0 / (HD ** 0.5)

    def one_group(which):
        query = lax.dynamic_index_in_dim(query_heads, which, 0, keepdims=False)
        row_vis = lax.dynamic_index_in_dim(visible, which, 0, keepdims=False)
        allow = (key_group == which) | ((key_group < which) & (row_vis[key_group] == 1))
        scores = jnp.einsum("qhd,khd->hqk", query.astype(jnp.float32), key_heads.astype(jnp.float32)) * scale
        scores = jnp.where(allow[None, None, :], scores, -jnp.inf)
        row_max = jnp.max(scores, axis=2)
        probs = jnp.exp(scores - row_max[..., None])
        row_total = jnp.sum(probs, axis=2)
        rounded = lax.optimization_barrier(probs.astype(jnp.bfloat16)).astype(jnp.float32)
        mixed = jnp.einsum("hqk,khd->hqd", rounded, value_heads.astype(jnp.float32))
        mixed = mixed / row_total[..., None]
        return jnp.transpose(mixed, (1, 0, 2)).reshape(TOK, HEADS * HD).astype(jnp.bfloat16)

    attended = lax.map(one_group, jnp.arange(GROUPS, dtype=jnp.int32))
    projected = jnp.dot(attended.reshape(GROUPS * TOK, HEADS * HD), out_weight, preferred_element_type=jnp.float32)
    gates = jnp.repeat(gate_table[levels], TOK, axis=0)
    updated = (hidden.astype(jnp.float32) + gates * projected).astype(jnp.bfloat16)
    return jnp.concatenate([updated[TOK:], incoming], axis=0)
```

```python
import functools
import math

import jax
import jax.numpy as jnp
from jax import lax
from jax.experimental import pallas as pl
from jax.experimental.pallas import tpu as pltpu
from jax.sharding import PartitionSpec as P

HD = 128
TOK = 128
NY, NZ = 4, 8
NX = 4
PAIRS = NY * NZ
LOCAL_HEADS = 5
MAIN_TEAM, EXTRA_TEAM = 6, 8
SLOTS = 6
BIG = 1e30
MESH = pl.DeviceIdType.MESH
VMEM = pl.BlockSpec(memory_space=pltpu.VMEM)
ANY = pl.BlockSpec(memory_space=pl.ANY)


def coords():
    p = lax.axis_index("group")
    hd = lax.axis_index("head")
    return p // NZ, p % NZ, hd // 2, hd % 2


def remote(src, dst, send, recv, p, hd):
    return pltpu.make_async_remote_copy(
        src_ref=src,
        dst_ref=dst,
        send_sem=send,
        recv_sem=recv,
        device_id=(p, hd),
        device_id_type=MESH,
    )


def team():
    y, z, x, c = coords()
    col = z % 4
    half = z // 4
    extra = y == col
    size = jnp.where(extra, EXTRA_TEAM, MAIN_TEAM)
    rank = jnp.where(extra, 2 * col + c, 2 * ((y - col - 1 + NY) % NY) + c)
    head = jnp.where(extra, 4, col)
    return extra, size, rank, half, head


def pair_of(slot, size, rank):
    pos = jnp.where(slot % 2 == 0, rank, size - 1 - rank)
    return PAIRS - 1 - (slot * size + pos)


def owner_of(pair, head, x, c):
    size = MAIN_TEAM if head < 4 else EXTRA_TEAM
    t = PAIRS - 1 - pair
    slot = t // size
    pos = t % size
    rank = jnp.where(slot % 2 == 0, pos, size - 1 - pos)
    chip = rank // 2
    if head < 4:
        yd, zd = (head + 1 + chip) % NY, 4 * c + head
    else:
        yd, zd = chip, 4 * c + chip
    return yd * NZ + zd, 2 * x + rank % 2, slot


def gather_kernel(
    q_ref, k_ref, v_ref, buf, qbuf, qt, vt, qsend, ksend, vsend, qrecv, rmain, rextra, rsib, snext, sprev, enext, eprev, ssib
):
    y, z, x, c = coords()
    p = y * NZ + z
    hd = 2 * x + c
    extra, size, rank, half, head_in = team()
    col = z % 4

    def put(src, dst, send, recv, pd, hdd):
        me = jnp.logical_and(pd == p, hdd == hd)

        @pl.when(me)
        def _():
            pltpu.make_async_copy(src, dst, recv).start()

        @pl.when(jnp.logical_not(me))
        def _():
            remote(src, dst, send, recv, pd, hdd).start()

    def put_done(src, dst, send, recv, pd, hdd):
        me = jnp.logical_and(pd == p, hdd == hd)

        @pl.when(jnp.logical_not(me))
        def _():
            remote(src, dst, send, recv, pd, hdd).wait_send()

    def k_args(h):
        zd = 4 * c + h if h < 4 else 4 * c + y
        idx = jnp.where(y == h, 2, 0) if h < 4 else 0
        sems = rmain if h < 4 else rextra
        return (k_ref.at[:, pl.ds(h * HD, HD)], buf.at[idx, p], ksend.at[h], sems.at[p], y * NZ + zd, 2 * x)

    def v_args(h):
        zd = 4 * c + h if h < 4 else 4 * c + y
        idx = jnp.where(y == h, 2, 1) if h < 4 else 1
        sems = rmain if h < 4 else rextra
        return (vt.at[h], buf.at[idx, p], vsend.at[h], sems.at[p], y * NZ + zd, 2 * x + 1)

    def q_args(h):
        pd, hdd, slot = owner_of(p, h, x, c)
        return (qt.at[h], qbuf.at[slot], qsend.at[h], qrecv.at[slot], pd, hdd)

    for h in range(LOCAL_HEADS):
        put(*k_args(h))
    for h in range(LOCAL_HEADS):
        for g in range(2):
            vt[h, g * TOK : (g + 1) * TOK, :] = v_ref[g * TOK : (g + 1) * TOK, h * HD : (h + 1) * HD].T
        put(*v_args(h))
    for h in range(LOCAL_HEADS):
        qt[h] = q_ref[:, h * HD : (h + 1) * HD].T
        put(*q_args(h))

    yn, yp, yo = (y + 1) % NY, (y + 3) % NY, (y + 2) % NY

    def ring(step, main):
        if main:
            mine = jnp.where(extra, 2, c)
            there = lambda yd: jnp.where(yd == col, 2, c)
            zn, zp = z, z
            sems, to_next, to_prev = rmain, snext, sprev
        else:
            mine = c
            there = lambda yd: c
            zn, zp = 4 * half + yn, 4 * half + yp
            sems, to_next, to_prev = rextra, enext, eprev
        pn, pp = yn * NZ + zn, yp * NZ + zp

        def arrive(i):
            remote(buf.at[mine, i], buf.at[mine, i], to_next.at[0], sems.at[i], pn, hd).wait_recv()

        def go_next(i, s):
            return remote(buf.at[mine, i], buf.at[there(yn), i], to_next.at[s], sems.at[i], pn, hd)

        def go_prev(i, s):
            return remote(buf.at[mine, i], buf.at[there(yp), i], to_prev.at[s], sems.at[i], pp, hd)

        def sibling(i):
            copy = remote(buf.at[c, i], buf.at[c, i], ssib.at[i], rsib.at[i], p, 2 * x + 1 - c)
            if main:

                @pl.when(jnp.logical_not(extra))
                def _():
                    copy.start()
            else:
                copy.start()

        def own(b, carry):
            i = y * NZ + b
            arrive(i)
            go_next(i, b).start()
            go_prev(i, b).start()
            sibling(i)
            return carry

        def forward(b, carry):
            i = yp * NZ + b
            arrive(i)
            go_next(i, 8 + b).start()
            sibling(i)
            i = yn * NZ + 4 + b
            arrive(i)
            go_prev(i, 8 + b).start()
            sibling(i)
            return carry

        def rest(b, carry):
            for i in (yp * NZ + 4 + b, yn * NZ + b, yo * NZ + b, yo * NZ + 4 + b):
                arrive(i)
                sibling(i)
            return carry

        def close(b, carry):
            go_next(b, b).wait_send()
            go_prev(b, b).wait_send()
            return carry

        if step == 0:
            lax.fori_loop(0, NZ, own, 0)
        elif step == 1:
            lax.fori_loop(0, 4, forward, 0)
        elif step == 2:
            lax.fori_loop(0, 4, rest, 0)
        else:
            lax.fori_loop(0, 12, close, 0)

    for step in range(4):
        ring(step, True)

        @pl.when(extra)
        def _():
            ring(step, False)

    def sib_done(i, carry):
        remote(buf.at[c, i], buf.at[c, i], ssib.at[i], rsib.at[i], p, 2 * x + 1 - c).wait_send()
        remote(buf.at[1 - c, i], buf.at[1 - c, i], ssib.at[i], rsib.at[i], p, 2 * x + 1 - c).wait_recv()
        return carry

    lax.fori_loop(0, PAIRS, sib_done, 0)
    for h in range(LOCAL_HEADS):
        put_done(*k_args(h))
        put_done(*v_args(h))
        put_done(*q_args(h))
    for slot in range(SLOTS):

        @pl.when(pair_of(slot, size, rank) >= 0)
        def _():
            remote(qt.at[0], qbuf.at[slot], qsend.at[0], qrecv.at[slot], p, hd).wait_recv()


def attend_kernel(kv_ref, q_ref, vis_ref, o_ref, bias):
    extra, size, rank, half, head = team()
    scale = math.log2(math.e) / math.sqrt(HD)
    seen = (vis_ref[...] == 1).astype(jnp.float32).astype(jnp.bfloat16)

    def one_slot(slot, carry):
        pair = pair_of(slot, size, rank)
        group = 2 * pair + (lax.broadcasted_iota(jnp.int32, (64, 2 * TOK), 1) >= TOK).astype(jnp.int32)
        row = lax.broadcasted_iota(jnp.int32, (64, 2 * TOK), 0)
        pick = (row == group).astype(jnp.float32).astype(jnp.bfloat16)
        here = lax.dot_general(seen, pick, (((0,), (0,)), ((), ())), preferred_element_type=jnp.float32)
        allow = (row == group) | ((row < group) & (here > 0.5))
        bias[...] = jnp.where(allow, 0.0, -BIG).reshape(16, 4, 2 * TOK)
        query = q_ref[slot]

        def step(j, state):
            row_max, row_total, acc = state
            keys = kv_ref[0, pl.ds(2 * j, 2)].reshape(512, HD)
            s = jnp.dot(keys, query, preferred_element_type=jnp.float32) * scale
            s = s.reshape(4, TOK, 2 * TOK) + bias[j].reshape(4, 1, 2 * TOK)
            new_max = jnp.maximum(row_max, jnp.max(jnp.max(s, axis=0), axis=0, keepdims=True))
            keep = jnp.exp2(row_max - new_max)
            probs = jnp.exp2(s - new_max.reshape(1, 1, 2 * TOK))
            row_total = row_total * keep + jnp.sum(jnp.sum(probs, axis=0), axis=0, keepdims=True)
            probs = probs.astype(jnp.bfloat16).reshape(512, 2 * TOK)
            values = jnp.concatenate(
                [kv_ref[1, 2 * j + b, g * TOK : (g + 1) * TOK, :] for b in range(2) for g in range(2)], axis=1
            )
            acc = acc * keep + jnp.dot(values, probs, preferred_element_type=jnp.float32)
            return new_max, row_total, acc

        state = (
            jnp.full((1, 2 * TOK), -BIG, jnp.float32),
            jnp.zeros((1, 2 * TOK), jnp.float32),
            jnp.zeros((HD, 2 * TOK), jnp.float32),
        )
        row_max, row_total, acc = lax.fori_loop(0, (pair + 2) // 2, step, state)
        mixed = acc / row_total
        for g in range(2):
            o_ref[slot, g] = mixed[:, g * TOK : (g + 1) * TOK].T.astype(jnp.bfloat16)
        return carry

    slots = jnp.where(extra, 4, jnp.where(rank >= 4, 6, 5))
    lax.fori_loop(0, slots, one_slot, 0)


def project_kernel(
    o_ref, w_ref, hid_ref, gate_ref, inc_ref, out_ref, att, w, s1, r1, s2, r2, hs, gs,
    wsem, osend, orecv, send1, recv1, send2, recv2, hsend, hrecv
):
    y, z, x, c = coords()
    p = y * NZ + z
    hd = 2 * x + c
    extra, size, rank, half, head = team()
    wcopy = pltpu.make_async_copy(w_ref, w, wsem)
    wcopy.start()

    shift = [
        remote(hid_ref.at[pl.ds(0, TOK)], hs, hsend.at[0], hrecv.at[0], p - 1, hd),
        remote(gate_ref.at[0], gs, hsend.at[1], hrecv.at[1], p - 1, hd),
    ]

    @pl.when(p > 0)
    def _():
        for copy in shift:
            copy.start()

    def o_args(slot, g):
        pair = pair_of(slot, size, rank)
        pd = pair - 1 + g
        dst = att.at[pl.ds((1 - g) * TOK, TOK), pl.ds(pl.multiple_of(head * HD, HD), HD)]
        return o_ref.at[slot, g], dst, osend.at[2 * slot + g], orecv.at[(1 - g) * LOCAL_HEADS + head], pd, 2 * x + half

    for slot in range(SLOTS):
        for g in range(2):
            src, dst, send, recv, pd, hdd = o_args(slot, g)
            me = jnp.logical_and(pd == p, hdd == hd)

            @pl.when(jnp.logical_and(pd >= 0, me))
            def _():
                pltpu.make_async_copy(src, dst, recv).start()

            @pl.when(jnp.logical_and(pd >= 0, jnp.logical_not(me)))
            def _():
                remote(src, dst, send, recv, pd, hdd).start()

    last = p == PAIRS - 1

    @pl.when(last)
    def _():
        att[TOK:, :] = jnp.zeros((TOK, LOCAL_HEADS * HD), jnp.bfloat16)

    def o_arrive(g, h):
        dst = att.at[pl.ds(g * TOK, TOK), pl.ds(h * HD, HD)]
        remote(dst, dst, osend.at[0], orecv.at[g * LOCAL_HEADS + h], p, hd).wait_recv()

    for h in range(LOCAL_HEADS):
        o_arrive(0, h)

    @pl.when(jnp.logical_not(last))
    def _():
        for h in range(LOCAL_HEADS):
            o_arrive(1, h)

    wcopy.wait()
    width = LOCAL_HEADS * HD
    offsets = (2, 1, 3, 0)

    def part(j, core):
        xd = (x + offsets[j]) % NX
        cols = pl.ds(pl.multiple_of((2 * xd + core) * width, HD), width)
        return jnp.dot(att[...], w[:, cols], preferred_element_type=jnp.float32)

    def across(j):
        return remote(s1.at[j], r1.at[j], send1.at[j], recv1.at[j], p, 2 * x + 1 - c)

    def along(j):
        xd = (x + offsets[j]) % NX
        return remote(s2.at[j], r2.at[j], send2.at[j], recv2.at[j], p, 2 * xd + c)

    for j in range(4):
        s1[j] = part(j, 1 - c).astype(jnp.bfloat16)
        across(j).start()
    for j in range(4):
        mine = part(j, c)
        across(j).wait_recv()
        mine = mine + r1[j].astype(jnp.float32)
        if j < 3:
            s2[j] = mine.astype(jnp.bfloat16)
            along(j).start()
    total = mine
    for j in (1, 2, 0):
        along(j).wait_recv()
        total = total + r2[j].astype(jnp.float32)

    out_ref[:TOK, :] = (hid_ref[TOK:, :].astype(jnp.float32) + gate_ref[1, 0:1, :] * total[:TOK]).astype(jnp.bfloat16)

    @pl.when(last)
    def _():
        out_ref[TOK:, :] = inc_ref[...]

    @pl.when(jnp.logical_not(last))
    def _():
        for copy in shift:
            copy.wait_recv()
        out_ref[TOK:, :] = (hs[...].astype(jnp.float32) + gs[0:1, :] * total[TOK:]).astype(jnp.bfloat16)

    @pl.when(p > 0)
    def _():
        for copy in shift:
            copy.wait_send()

    for j in range(4):
        across(j).wait_send()
        if j < 3:
            along(j).wait_send()
    for slot in range(SLOTS):
        for g in range(2):
            src, dst, send, recv, pd, hdd = o_args(slot, g)
            me = jnp.logical_and(pd == p, hdd == hd)

            @pl.when(jnp.logical_and(pd >= 0, jnp.logical_not(me)))
            def _():
                remote(src, dst, send, recv, pd, hdd).wait_send()


def on_device(query_states, key_states, value_states, hidden, out_weight, gate_table, levels, visible, incoming):
    dma = pltpu.SemaphoreType.DMA
    bf16 = jnp.bfloat16
    width = LOCAL_HEADS * HD
    rows = 2 * TOK
    kv, queries = pl.pallas_call(
        gather_kernel,
        out_shape=(
            jax.ShapeDtypeStruct((3, PAIRS, rows, HD), bf16),
            jax.ShapeDtypeStruct((SLOTS, HD, rows), bf16),
        ),
        in_specs=[VMEM] * 3,
        out_specs=(VMEM, VMEM),
        scratch_shapes=[
            pltpu.VMEM((LOCAL_HEADS, HD, rows), bf16),
            pltpu.VMEM((LOCAL_HEADS, rows, HD), bf16),
            dma((5,)),
            dma((5,)),
            dma((5,)),
            dma((SLOTS,)),
            dma((PAIRS,)),
            dma((PAIRS,)),
            dma((PAIRS,)),
            dma((12,)),
            dma((12,)),
            dma((12,)),
            dma((12,)),
            dma((PAIRS,)),
        ],
        compiler_params=pltpu.CompilerParams(has_side_effects=True, vmem_limit_bytes=40 << 20),
        name="gather",
    )(query_states, key_states, value_states)

    attended = pl.pallas_call(
        attend_kernel,
        out_shape=jax.ShapeDtypeStruct((SLOTS, 2, TOK, HD), bf16),
        grid=(1,),
        in_specs=[
            pl.BlockSpec((2, PAIRS, rows, HD), lambda i: (0, 0, 0, 0)),
            pl.BlockSpec((SLOTS, HD, rows), lambda i: (0, 0, 0)),
            pl.BlockSpec((64, 64), lambda i: (0, 0)),
        ],
        out_specs=pl.BlockSpec((SLOTS, 2, TOK, HD), lambda i: (0, 0, 0, 0)),
        scratch_shapes=[pltpu.VMEM((16, 4, rows), jnp.float32)],
        compiler_params=pltpu.CompilerParams(vmem_limit_bytes=40 << 20),
        name="attend",
    )(kv, queries, visible)

    gates = jnp.concatenate([lax.dynamic_slice_in_dim(gate_table, levels[g], 1, 0) for g in range(2)], axis=0)
    gates = jnp.broadcast_to(gates[:, None, :], (2, 8, width))
    return pl.pallas_call(
        project_kernel,
        out_shape=jax.ShapeDtypeStruct((rows, width), bf16),
        in_specs=[VMEM, ANY, VMEM, VMEM, VMEM],
        out_specs=VMEM,
        scratch_shapes=[
            pltpu.VMEM((rows, width), bf16),
            pltpu.VMEM((width, 8 * width), bf16),
            pltpu.VMEM((4, rows, width), bf16),
            pltpu.VMEM((4, rows, width), bf16),
            pltpu.VMEM((3, rows, width), bf16),
            pltpu.VMEM((3, rows, width), bf16),
            pltpu.VMEM((TOK, width), bf16),
            pltpu.VMEM((8, width), jnp.float32),
            dma(()),
            dma((2 * SLOTS,)),
            dma((2 * LOCAL_HEADS,)),
            dma((4,)),
            dma((4,)),
            dma((3,)),
            dma((3,)),
            dma((2,)),
            dma((2,)),
        ],
        compiler_params=pltpu.CompilerParams(has_side_effects=True, vmem_limit_bytes=40 << 20),
        name="project",
    )(attended, out_weight, hidden, gates, incoming)


def solution(mesh):
    return jax.shard_map(
        on_device,
        mesh=mesh,
        in_specs=(
            P("group", "head"),
            P("group", "head"),
            P("group", "head"),
            P("group", "head"),
            P("head", None),
            P(None, "head"),
            P("group"),
            P(),
            P(None, "head"),
        ),
        out_specs=P("group", "head"),
        check_vma=False,
    )
```

```python
import math

import jax
import jax.numpy as jnp
from jax import lax
from jax.experimental import pallas as pl
from jax.experimental.pallas import tpu as pltpu
from jax.sharding import PartitionSpec as P

HD = 128
TOK = 128
ROWS = 2 * TOK
NY, NZ, NX = 4, 8, 4
PAIRS = NY * NZ
HEADS = 5
WIDTH = HEADS * HD
LEVELS = 1000
MAIN_TEAM, EXTRA_TEAM = 6, 8
SLOTS = 6
CHUNK = 4
KEYS = CHUNK * ROWS
PARTS = 2 * CHUNK
PER_QUARTER = NZ // CHUNK
MASKED = -1e30
LOWEST = -1e20
MESH = pl.DeviceIdType.MESH
ANY = pl.BlockSpec(memory_space=pl.ANY)
bf16 = jnp.bfloat16
f32 = jnp.float32


def remote(src, dst, send, recv, p, hd):
    return pltpu.make_async_remote_copy(
        src_ref=src, dst_ref=dst, send_sem=send, recv_sem=recv, device_id=(p, hd), device_id_type=MESH
    )


def unless(cond):
    return pl.when(jnp.logical_not(cond))


def pair_of(slot, size, rank):
    pos = jnp.where(slot % 2 == 0, rank, size - 1 - rank)
    return PAIRS - 1 - (slot * size + pos)


def owner_of(pair, head, x, c):
    size = MAIN_TEAM if head < 4 else EXTRA_TEAM
    t = PAIRS - 1 - pair
    slot = t // size
    pos = t % size
    rank = jnp.where(slot % 2 == 0, pos, size - 1 - pos)
    chip = rank // 2
    if head < 4:
        return ((x + 1 + chip) % NY) * NZ + 4 * c + head, 2 * x + rank % 2, slot
    return chip * NZ + 2 * x + c, 2 * chip + rank % 2, slot


def body(
    q_hbm, k_hbm, v_hbm, hid_hbm, w_hbm, gate_hbm, levels, vis_hbm, inc_hbm, out_ref,
    q_in, k_in, v_in, hid, w, gate, vis, inc, buf, qbuf, qt, vt, bias, s_a, s_b, p_a, p_b, keep_a, keep_b,
    row_max, acc, o_buf, att, s1, r1, far, far_in, near, near_in, hs, gs, gs_out,
    lsem, qsend, ksend, vsend, qrecv, rmain, rextra, rsib, snext, sprev, enext, eprev, ssib,
    osend, orecv, send1, recv1, fsend, frecv, nsend, nrecv, hsend, hrecv
):
    p = lax.axis_index("group")
    hd = lax.axis_index("head")
    y, z, x, c = p // NZ, p % NZ, hd // 2, hd % 2
    sib = 2 * x + 1 - c
    half, col = z // 4, z % 4
    extra = y == x
    last = p == PAIRS - 1
    size = jnp.where(extra, EXTRA_TEAM, MAIN_TEAM)
    rank = jnp.where(extra, 2 * x + c, 2 * ((y - x - 1 + NY) % NY) + c)
    head = jnp.where(extra, 4, col)
    home = jnp.where(extra, z, 2 * x + half)
    pairs = [pair_of(slot, size, rank) for slot in range(SLOTS)]
    yn, yp, yo = (y + 1) % NY, (y + 3) % NY, (y + 2) % NY

    def is_me(pd, hdd):
        return jnp.logical_and(pd == p, hdd == hd)

    loads = [
        pltpu.make_async_copy(src, dst, lsem.at[i])
        for i, (src, dst) in enumerate(
            [(k_hbm, k_in), (v_hbm, v_in), (q_hbm, q_in), (hid_hbm, hid), (vis_hbm, vis), (gate_hbm, gate), (w_hbm, w), (inc_hbm, inc)]
        )
    ]
    for copy in loads:
        copy.start()

    barrier = pltpu.get_barrier_semaphore()

    def ready(pd, hdd):
        pl.semaphore_signal(barrier, inc=1, device_id=(pd, hdd), device_id_type=MESH)

    def ready_unless_me(pd, hdd):
        @unless(is_me(pd, hdd))
        def _():
            ready(pd, hdd)

    for dz in range(NZ):
        ready_unless_me(y * NZ + dz, 2 * x + half)
    ready(yn * NZ + z, hd)
    ready(yp * NZ + z, hd)
    ready(p, sib)

    @pl.when(extra)
    def _():
        for dz in range(NZ):
            ready_unless_me(y * NZ + dz, z)
        ready(yn * NZ + z, 2 * yn + c)
        ready(yp * NZ + z, 2 * yp + c)

    for slot in range(SLOTS):

        @pl.when(pairs[slot] >= 0)
        def _():
            ready_unless_me(pairs[slot], home)

    for h in range(HEADS):
        pd, hdd, _ = owner_of(p, h, x, c)
        ready_unless_me(pd, hdd)

    @unless(last)
    def _():
        for h in range(HEADS):
            pd, hdd, _ = owner_of(p + 1, h, x, c)
            ready_unless_me(pd, hdd)
        ready(p + 1, hd)

    xn, xp, xo = (x + 1) % NX, (x + 3) % NX, (x + 2) % NX
    ready(p, 2 * xn + c)
    ready(p, 2 * xp + c)

    def count(flag):
        return flag.astype(jnp.int32)

    def others(pd, hdd):
        return 1 - count(is_me(pd, hdd))

    expected = 2 + 1 + 2 + jnp.where(extra, 2, 0) + count(p > 0)
    for k in range(2):
        for h in range(4):
            expected = expected + others(y * NZ + 4 * c + h, 2 * x + k)
        expected = expected + others(y * NZ + hd, 2 * y + k)
    for h in range(HEADS):
        pd, hdd, _ = owner_of(p, h, x, c)
        expected = expected + others(pd, hdd)
    for slot in range(SLOTS):
        for g in range(2):
            expected = expected + jnp.where(pairs[slot] - 1 + g >= 0, others(pairs[slot] - 1 + g, home), 0)

    def put(src, dst, send, recv, pd, hdd):
        @pl.when(is_me(pd, hdd))
        def _():
            pltpu.make_async_copy(src, dst, recv).start()

        @unless(is_me(pd, hdd))
        def _():
            remote(src, dst, send, recv, pd, hdd).start()

    def put_done(src, dst, send, recv, pd, hdd):
        @unless(is_me(pd, hdd))
        def _():
            remote(src, dst, send, recv, pd, hdd).wait_send()

    def kv_args(h, k):
        src = k_in.at[:, pl.ds(h * HD, HD)] if k == 0 else vt.at[h]
        send = ksend.at[h] if k == 0 else vsend.at[h]
        if h < 4:
            return src, buf.at[jnp.where(y == x, 2, k), p], send, rmain.at[p], y * NZ + 4 * c + h, 2 * x + k
        return src, buf.at[k, p], send, rextra.at[p], y * NZ + hd, 2 * y + k

    def q_args(h):
        pd, hdd, slot = owner_of(p, h, x, c)
        return qt.at[h], qbuf.at[slot], qsend.at[h], qrecv.at[slot], pd, hdd

    for i in range(3):
        loads[i].wait()
    for h in range(HEADS):
        for g in range(2):
            vt[h, g * TOK : (g + 1) * TOK, :] = v_in[g * TOK : (g + 1) * TOK, h * HD : (h + 1) * HD].T
        qt[h] = q_in[:, h * HD : (h + 1) * HD].T
    for slot in range(3, SLOTS):

        @pl.when(pairs[slot] < 0)
        def _():
            qbuf[slot] = jnp.zeros((HD, ROWS), bf16)

    @pl.when(last)
    def _():
        att[TOK:, :] = jnp.zeros((TOK, WIDTH), bf16)

    pl.semaphore_wait(barrier, expected)

    for h in range(HEADS):
        for k in range(2):
            put(*kv_args(h, k))
    for h in range(HEADS):
        put(*q_args(h))

    for i in range(3, 6):
        loads[i].wait()
    gs_out[...] = jnp.broadcast_to(gate[pl.ds(levels[0], 1), :], (8, WIDTH))
    shift = [
        remote(hid.at[pl.ds(0, TOK)], hs, hsend.at[0], hrecv.at[0], p - 1, hd),
        remote(gs_out, gs, hsend.at[1], hrecv.at[1], p - 1, hd),
    ]

    @pl.when(p > 0)
    def _():
        for copy in shift:
            copy.start()

    seen = (vis[...] == 1).astype(f32).astype(bf16)
    key_group = lax.broadcasted_iota(jnp.int32, (64, ROWS), 0)
    second = (lax.broadcasted_iota(jnp.int32, (64, ROWS), 1) >= TOK).astype(jnp.int32)
    for slot in range(SLOTS):
        group = 2 * pairs[slot] + second
        pick = (key_group == group).astype(f32).astype(bf16)
        here = lax.dot_general(seen, pick, (((0,), (0,)), ((), ())), preferred_element_type=f32)
        allow = (key_group == group) | ((key_group < group) & (here > 0.5))
        bias[slot] = jnp.where(allow, 0.0, MASKED).reshape(PAIRS // CHUNK, PARTS, ROWS)
        row_max[slot] = jnp.full((8, ROWS), LOWEST, f32)
        acc[slot] = jnp.zeros((HD + 16, ROWS), f32)

    def sibling(i):
        return remote(buf.at[c, i], buf.at[c, i], ssib.at[i], rsib.at[i], p, sib)

    def ring(step, main):
        if main:
            mine = jnp.where(extra, 2, c)
            there_n, there_p = jnp.where(yn == x, 2, c), jnp.where(yp == x, 2, c)
            hn, hp = hd, hd
            sems, to_next, to_prev = rmain, snext, sprev
        else:
            mine, there_n, there_p = c, c, c
            hn, hp = 2 * yn + c, 2 * yp + c
            sems, to_next, to_prev = rextra, enext, eprev
        pn, pp = yn * NZ + z, yp * NZ + z

        def arrive(i):
            remote(buf.at[mine, i], buf.at[mine, i], to_next.at[0], sems.at[i], pn, hn).wait_recv()

        def go_next(i, s):
            return remote(buf.at[mine, i], buf.at[there_n, i], to_next.at[s], sems.at[i], pn, hn)

        def go_prev(i, s):
            return remote(buf.at[mine, i], buf.at[there_p, i], to_prev.at[s], sems.at[i], pp, hp)

        def across(i):
            if main:

                @unless(extra)
                def _():
                    sibling(i).start()
            else:
                sibling(i).start()

        def own(b, carry):
            i = y * NZ + b
            arrive(i)
            go_next(i, b).start()
            go_prev(i, b).start()
            across(i)
            return carry

        def forward(b, carry):
            i = yp * NZ + b
            arrive(i)
            go_next(i, 8 + b).start()
            across(i)
            i = yn * NZ + 4 + b
            arrive(i)
            go_prev(i, 8 + b).start()
            across(i)
            return carry

        def rest(b, carry):
            for i in (yp * NZ + 4 + b, yn * NZ + b):
                arrive(i)
                across(i)
            return carry

        def far_side(b, carry):
            i = yo * NZ + b
            arrive(i)
            across(i)
            return carry

        def close(b, carry):
            go_next(b, b).wait_send()
            go_prev(b, b).wait_send()
            return carry

        if step == 0:
            lax.fori_loop(0, NZ, own, 0)
        elif step == 1:
            lax.fori_loop(0, 4, forward, 0)
        elif step == 2:
            lax.fori_loop(0, 4, rest, 0)
        elif step == 3:
            lax.fori_loop(0, NZ, far_side, 0)
        else:
            lax.fori_loop(0, 12, close, 0)

    def rings(step):
        ring(step, True)

        @pl.when(extra)
        def _():
            ring(step, False)

    def from_sibling(quarter):
        def one(b, carry):
            i = quarter * NZ + b
            remote(buf.at[1 - c, i], buf.at[1 - c, i], ssib.at[i], rsib.at[i], p, sib).wait_recv()
            return carry

        lax.fori_loop(0, NZ, one, 0)

    ones = jnp.ones((16, KEYS), bf16)
    scale = math.log2(math.e) / math.sqrt(HD)

    def attend(quarter):
        ends = []
        total = 0
        for slot in range(SLOTS):
            total = total + jnp.clip((pairs[slot] + 1 - NZ * quarter + CHUNK - 1) // CHUNK, 0, PER_QUARTER)
            ends.append(total)

        def item(i):
            slot, base = 0, 0
            for s in range(SLOTS - 1):
                past = i >= ends[s]
                slot = slot + past.astype(jnp.int32)
                base = jnp.where(past, ends[s], base)
            return slot, quarter * PER_QUARTER + jnp.clip(i - base, 0, PER_QUARTER - 1), i < total

        def score(i, s):
            slot, chunk, _ = item(i)
            keys = buf[0, pl.ds(CHUNK * chunk, CHUNK)].reshape(KEYS, HD)
            s[...] = jnp.dot(keys, qbuf[slot], preferred_element_type=f32)

        def weigh(i, probs, keep):
            slot, chunk, _ = item(i)
            values = jnp.concatenate(
                [buf[1, CHUNK * chunk + b, g * TOK : (g + 1) * TOK, :] for b in range(CHUNK) for g in range(2)], axis=1
            )
            values = jnp.concatenate([values, ones], axis=0)
            acc[slot] = acc[slot] * keep[0:1] + jnp.dot(values, probs[...], preferred_element_type=f32)

        def soften(i, s, probs, keep):
            slot, chunk, valid = item(i)
            offset = bias[slot, chunk] + jnp.where(valid, 0.0, MASKED)
            old = row_max[slot, 0:1]
            new = old
            for g in range(PARTS):
                top = jnp.max(s[g * TOK : (g + 1) * TOK, :], axis=0, keepdims=True)
                new = jnp.maximum(new, top * scale + offset[g : g + 1])
            keep[...] = jnp.broadcast_to(jnp.exp2(old - new), (8, ROWS))
            row_max[slot] = jnp.broadcast_to(new, (8, ROWS))
            for g in range(PARTS):
                t = s[g * TOK : (g + 1) * TOK, :] * scale + (offset[g : g + 1] - new)
                probs[g * TOK : (g + 1) * TOK, :] = jnp.exp2(t).astype(bf16)

        score(0, s_a)
        p_b[...] = jnp.zeros_like(p_b)
        keep_b[...] = jnp.ones_like(keep_b)

        def two(n, carry):
            i = 2 * n
            weigh(jnp.maximum(i - 1, 0), p_b, keep_b)
            score(i + 1, s_b)
            soften(i, s_a, p_a, keep_a)
            weigh(i, p_a, keep_a)
            score(i + 2, s_a)
            soften(i + 1, s_b, p_b, keep_b)
            return carry

        turns = (total + 1) // 2
        lax.fori_loop(0, turns, two, 0)

        @pl.when(turns > 0)
        def _():
            weigh(2 * turns - 1, p_b, keep_b)

    rings(0)
    rings(1)
    from_sibling(y)
    for slot in range(SLOTS):

        @pl.when(pairs[slot] >= 0)
        def _():
            remote(qt.at[0], qbuf.at[slot], qsend.at[0], qrecv.at[slot], p, hd).wait_recv()

    attend(y)
    rings(2)
    from_sibling(yp)
    attend(yp)
    from_sibling(yn)
    attend(yn)
    rings(3)
    from_sibling(yo)
    attend(yo)

    def o_args(slot, g):
        pd = pairs[slot] - 1 + g
        dst = att.at[pl.ds((1 - g) * TOK, TOK), pl.ds(pl.multiple_of(head * HD, HD), HD)]
        return o_buf.at[slot, g], dst, osend.at[2 * slot + g], orecv.at[(1 - g) * HEADS + head], pd, home

    for slot in range(SLOTS):

        @pl.when(pairs[slot] >= 0)
        def _():
            mixed = acc[slot, :HD] / acc[slot, HD : HD + 1]
            for g in range(2):
                o_buf[slot, g] = mixed[:, g * TOK : (g + 1) * TOK].T.astype(bf16)
            put(*o_args(slot, 1))

        @pl.when(pairs[slot] >= 1)
        def _():
            put(*o_args(slot, 0))

    def o_arrive(g):
        for h in range(HEADS):
            dst = att.at[pl.ds(g * TOK, TOK), pl.ds(h * HD, HD)]
            remote(dst, dst, osend.at[0], orecv.at[g * HEADS + h], p, hd).wait_recv()

    o_arrive(0)

    @unless(last)
    def _():
        o_arrive(1)

    loads[6].wait()
    loads[7].wait()

    def part(xd, core):
        cols = pl.ds(pl.multiple_of((2 * xd + core) * WIDTH, HD), WIDTH)
        return jnp.dot(att[...], w[:, cols], preferred_element_type=f32)

    turn = (xo, xn, xp, x)

    def over(j):
        return remote(s1.at[j], r1.at[j], send1.at[j], recv1.at[j], p, sib)

    def far_copy(d):
        return remote(far.at[pl.ds(d * TOK, TOK)], far_in.at[d], fsend.at[d], frecv.at[d], p, 2 * (xn, xp)[d] + c)

    def near_copy(d):
        return remote(near.at[d], near_in.at[d], nsend.at[d], nrecv.at[d], p, 2 * (xn, xp)[d] + c)

    for j in range(4):
        s1[j] = part(turn[j], 1 - c).astype(bf16)
        over(j).start()

    def both(j):
        mine = part(turn[j], c)
        over(j).wait_recv()
        return mine + r1[j].astype(f32)

    far[...] = both(0).astype(bf16)
    far_copy(0).start()
    far_copy(1).start()
    for d in range(2):
        mine = both(1 + d)
        far_copy(d).wait_recv()
        near[d, (1 - d) * TOK : (2 - d) * TOK] = mine[(1 - d) * TOK : (2 - d) * TOK].astype(bf16)
        rows = slice(d * TOK, (d + 1) * TOK)
        near[d, rows] = (mine[rows] + far_in[d].astype(f32)).astype(bf16)
        near_copy(d).start()
    summed = both(3)
    for d in range(2):
        near_copy(d).wait_recv()
        summed = summed + near_in[d].astype(f32)

    out_ref[:TOK, :] = (hid[TOK:, :].astype(f32) + gate[pl.ds(levels[1], 1), :] * summed[:TOK]).astype(bf16)

    @pl.when(last)
    def _():
        out_ref[TOK:, :] = inc[...]

    @unless(last)
    def _():
        for copy in shift:
            copy.wait_recv()
        out_ref[TOK:, :] = (hs[...].astype(f32) + gs[0:1, :] * summed[TOK:]).astype(bf16)

    @pl.when(p > 0)
    def _():
        for copy in shift:
            copy.wait_send()

    for h in range(HEADS):
        for k in range(2):
            put_done(*kv_args(h, k))
        put_done(*q_args(h))
    rings(4)

    def sibling_done(i, carry):
        sibling(i).wait_send()
        return carry

    lax.fori_loop(0, PAIRS, sibling_done, 0)
    for slot in range(SLOTS):

        @pl.when(pairs[slot] >= 0)
        def _():
            put_done(*o_args(slot, 1))

        @pl.when(pairs[slot] >= 1)
        def _():
            put_done(*o_args(slot, 0))

    for j in range(4):
        over(j).wait_send()
    for d in range(2):
        far_copy(d).wait_send()
        near_copy(d).wait_send()


def on_device(query_states, key_states, value_states, hidden, out_weight, gate_table, levels, visible, incoming):
    dma = pltpu.SemaphoreType.DMA
    vmem = pltpu.VMEM
    return pl.pallas_call(
        body,
        out_shape=jax.ShapeDtypeStruct((ROWS, WIDTH), bf16),
        in_specs=[ANY] * 6 + [pl.BlockSpec(memory_space=pltpu.SMEM)] + [ANY] * 2,
        out_specs=pl.BlockSpec(memory_space=pltpu.VMEM),
        scratch_shapes=[
            vmem((ROWS, WIDTH), bf16),
            vmem((ROWS, WIDTH), bf16),
            vmem((ROWS, WIDTH), bf16),
            vmem((ROWS, WIDTH), bf16),
            vmem((WIDTH, 8 * WIDTH), bf16),
            vmem((LEVELS, WIDTH), f32),
            vmem((64, 64), jnp.int32),
            vmem((TOK, WIDTH), bf16),
            vmem((3, PAIRS, ROWS, HD), bf16),
            vmem((SLOTS, HD, ROWS), bf16),
            vmem((HEADS, HD, ROWS), bf16),
            vmem((HEADS, ROWS, HD), bf16),
            vmem((SLOTS, PAIRS // CHUNK, PARTS, ROWS), f32),
            vmem((KEYS, ROWS), f32),
            vmem((KEYS, ROWS), f32),
            vmem((KEYS, ROWS), bf16),
            vmem((KEYS, ROWS), bf16),
            vmem((8, ROWS), f32),
            vmem((8, ROWS), f32),
            vmem((SLOTS, 8, ROWS), f32),
            vmem((SLOTS, HD + 16, ROWS), f32),
            vmem((SLOTS, 2, TOK, HD), bf16),
            vmem((ROWS, WIDTH), bf16),
            vmem((4, ROWS, WIDTH), bf16),
            vmem((4, ROWS, WIDTH), bf16),
            vmem((ROWS, WIDTH), bf16),
            vmem((2, TOK, WIDTH), bf16),
            vmem((2, ROWS, WIDTH), bf16),
            vmem((2, ROWS, WIDTH), bf16),
            vmem((TOK, WIDTH), bf16),
            vmem((8, WIDTH), f32),
            vmem((8, WIDTH), f32),
            dma((8,)),
            dma((5,)),
            dma((5,)),
            dma((5,)),
            dma((SLOTS,)),
            dma((PAIRS,)),
            dma((PAIRS,)),
            dma((PAIRS,)),
            dma((12,)),
            dma((12,)),
            dma((12,)),
            dma((12,)),
            dma((PAIRS,)),
            dma((2 * SLOTS,)),
            dma((2 * HEADS,)),
            dma((4,)),
            dma((4,)),
            dma((2,)),
            dma((2,)),
            dma((2,)),
            dma((2,)),
            dma((2,)),
            dma((2,)),
        ],
        compiler_params=pltpu.CompilerParams(has_side_effects=True, collective_id=0, vmem_limit_bytes=56 << 20),
        name="block",
    )(query_states, key_states, value_states, hidden, out_weight, gate_table, levels, visible, incoming)


def solution(mesh):
    return jax.shard_map(
        on_device,
        mesh=mesh,
        in_specs=(
            P("group", "head"),
            P("group", "head"),
            P("group", "head"),
            P("group", "head"),
            P("head", None),
            P(None, "head"),
            P("group"),
            P(),
            P(None, "head"),
        ),
        out_specs=P("group", "head"),
        check_vma=False,
    )
```

```python
import math

import jax
import jax.numpy as jnp
from jax import lax
from jax.experimental import pallas as pl
from jax.experimental.pallas import tpu as pltpu
from jax.sharding import PartitionSpec as P

HD = 128
TOK = 128
ROWS = 2 * TOK
NY, NZ, NX = 4, 8, 4
PAIRS = NY * NZ
HEADS = 5
WIDTH = HEADS * HD
LEVELS = 1000
MAIN_TEAM, EXTRA_TEAM = 6, 8
SLOTS = 6
CHUNK = 4
KEYS = CHUNK * ROWS
PARTS = 2 * CHUNK
PER_QUARTER = NZ // CHUNK
AHEAD = 4
MASKED = -1e30
LOWEST = -1e20
MESH = pl.DeviceIdType.MESH
ANY = pl.BlockSpec(memory_space=pl.ANY)
bf16 = jnp.bfloat16
f32 = jnp.float32


def remote(src, dst, send, recv, p, hd):
    return pltpu.make_async_remote_copy(
        src_ref=src, dst_ref=dst, send_sem=send, recv_sem=recv, device_id=(p, hd), device_id_type=MESH
    )


def unless(cond):
    return pl.when(jnp.logical_not(cond))


def pair_of(slot, size, rank):
    pos = jnp.where(slot % 2 == 0, rank, size - 1 - rank)
    return PAIRS - 1 - (slot * size + pos)


def owner_of(pair, head, x, c):
    size = MAIN_TEAM if head < 4 else EXTRA_TEAM
    t = PAIRS - 1 - pair
    slot = t // size
    pos = t % size
    rank = jnp.where(slot % 2 == 0, pos, size - 1 - pos)
    chip = rank // 2
    if head < 4:
        return ((head + 1 + chip) % NY) * NZ + 4 * c + head, 2 * x + rank % 2, slot
    return x * NZ + x + 4 * c, 2 * chip + rank % 2, slot


def body(
    q_hbm, k_hbm, v_hbm, hid_hbm, w_hbm, gate_hbm, levels, vis_hbm, inc_hbm, out_ref,
    q_in, k_in, v_in, hid, w, gate, vis, inc, buf, qbuf, qt, vt, bias, s_a, s_b, p_a, p_b, keep_a, keep_b,
    row_max, acc, o_buf, att, s1, r1, far, far_in, near, near_in, keep, hs, gs, gs_out,
    lsem, qsend, ksend, vsend, qrecv, rmain, rextra, rsib, snext, sprev, enext, eprev, ssib,
    osend, orecv, send1, recv1, fsend, frecv, nsend, nrecv, hsend, hrecv
):
    p = lax.axis_index("group")
    hd = lax.axis_index("head")
    y, z, x, c = p // NZ, p % NZ, hd // 2, hd % 2
    sib = 2 * x + 1 - c
    half, col = z // 4, z % 4
    extra = y == col
    last = p == PAIRS - 1
    size = jnp.where(extra, EXTRA_TEAM, MAIN_TEAM)
    rank = jnp.where(extra, 2 * x + c, 2 * ((y - col - 1 + NY) % NY) + c)
    head = jnp.where(extra, 4, col)
    home = jnp.where(extra, 2 * col, 2 * x) + half
    pairs = [pair_of(slot, size, rank) for slot in range(SLOTS)]
    yn, yp, yo = (y + 1) % NY, (y + 3) % NY, (y + 2) % NY
    xn, xp, xo = (x + 1) % NX, (x + 3) % NX, (x + 2) % NX
    near_extra, far_extra = yn == col, yp == col
    order = [jnp.where(extra, a, b) for a, b in ((x, y), (xp, yp), (xn, yn), (xo, yo))]

    def is_me(pd, hdd):
        return jnp.logical_and(pd == p, hdd == hd)

    loads = [
        pltpu.make_async_copy(src, dst, lsem.at[i])
        for i, (src, dst) in enumerate(
            [(k_hbm, k_in), (v_hbm, v_in), (q_hbm, q_in), (hid_hbm, hid), (vis_hbm, vis), (gate_hbm, gate), (w_hbm, w), (inc_hbm, inc)]
        )
    ]
    for copy in loads:
        copy.start()

    barrier = pltpu.get_barrier_semaphore()

    def ready(pd, hdd):
        pl.semaphore_signal(barrier, inc=1, device_id=(pd, hdd), device_id_type=MESH)

    def ready_unless_me(pd, hdd):
        @unless(is_me(pd, hdd))
        def _():
            ready(pd, hdd)

    for dz in range(NZ):
        ready_unless_me(y * NZ + dz, 2 * x + half)
    ready(yn * NZ + z, hd)
    ready(yp * NZ + z, hd)
    ready(p, sib)
    ready(p, 2 * xn + c)
    ready(p, 2 * xp + c)

    @pl.when(extra)
    def _():
        for dz in range(NZ):
            ready_unless_me(x * NZ + dz, home)

    for slot in range(SLOTS):

        @pl.when(pairs[slot] >= 0)
        def _():
            ready_unless_me(pairs[slot], home)

    @unless(last)
    def _():
        ready(p + 1, hd)

    def count(flag):
        return flag.astype(jnp.int32)

    def others(pd, hdd):
        return 1 - count(is_me(pd, hdd))

    expected = 2 + 1 + 2 + count(p > 0)
    for k in range(2):
        for h in range(4):
            expected = expected + others(y * NZ + 4 * c + h, 2 * x + k)
        expected = expected + others(x * NZ + x + 4 * c, 2 * y + k)
    for h in range(HEADS):
        pd, hdd, _ = owner_of(p, h, x, c)
        expected = expected + others(pd, hdd)

    def put(src, dst, send, recv, pd, hdd):
        @pl.when(is_me(pd, hdd))
        def _():
            pltpu.make_async_copy(src, dst, recv).start()

        @unless(is_me(pd, hdd))
        def _():
            remote(src, dst, send, recv, pd, hdd).start()

    def put_done(src, dst, send, recv, pd, hdd):
        @unless(is_me(pd, hdd))
        def _():
            remote(src, dst, send, recv, pd, hdd).wait_send()

    def main_args(h, k):
        src = k_in.at[:, pl.ds(pl.multiple_of(h * HD, HD), HD)] if k == 0 else vt.at[h]
        send = ksend.at[h] if k == 0 else vsend.at[h]
        return src, buf.at[jnp.where(y == h, 2, k), p], send, rmain.at[p], y * NZ + 4 * c + h, 2 * x + k

    def extra_args(k):
        src = k_in.at[:, pl.ds(4 * HD, HD)] if k == 0 else vt.at[4]
        send = ksend.at[4] if k == 0 else vsend.at[4]
        return src, buf.at[k, p], send, rextra.at[p], x * NZ + x + 4 * c, 2 * y + k

    def q_args(h):
        pd, hdd, slot = owner_of(p, h, x, c)
        return qt.at[h], qbuf.at[slot], qsend.at[h], qrecv.at[slot], pd, hdd

    for i in range(2):
        loads[i].wait()
    for h in range(HEADS):
        for g in range(2):
            vt[h, g * TOK : (g + 1) * TOK, :] = v_in[g * TOK : (g + 1) * TOK, h * HD : (h + 1) * HD].T
    for slot in range(3, SLOTS):

        @pl.when(pairs[slot] < 0)
        def _():
            qbuf[slot] = jnp.zeros((HD, ROWS), bf16)

    @pl.when(last)
    def _():
        att[TOK:, :] = jnp.zeros((TOK, WIDTH), bf16)

    pl.semaphore_wait(barrier, expected)

    def away(n):
        return (z + jnp.where(n % 2 == 1, (n + 1) // 2, NZ - n // 2)) % NZ

    def issue(n):
        zd = away(n)

        @pl.when(zd // 4 == c)
        def _():
            for k in range(2):
                put(*main_args(zd % 4, k))

        @pl.when(zd == x + 4 * c)
        def _():
            for k in range(2):
                put(*extra_args(k))

    for n in range(AHEAD):
        issue(n)
    loads[2].wait()
    for h in range(HEADS):
        qt[h] = q_in[:, h * HD : (h + 1) * HD].T

    for i in range(3, 6):
        loads[i].wait()
    gs_out[...] = jnp.broadcast_to(gate[pl.ds(levels[0], 1), :], (8, WIDTH))
    shift = [
        remote(hid.at[pl.ds(0, TOK)], hs, hsend.at[0], hrecv.at[0], p - 1, hd),
        remote(gs_out, gs, hsend.at[1], hrecv.at[1], p - 1, hd),
    ]

    @pl.when(p > 0)
    def _():
        for copy in shift:
            copy.start()

    seen = (vis[...] == 1).astype(f32).astype(bf16)
    key_group = lax.broadcasted_iota(jnp.int32, (64, ROWS), 0)
    second = (lax.broadcasted_iota(jnp.int32, (64, ROWS), 1) >= TOK).astype(jnp.int32)
    for slot in range(SLOTS):
        group = 2 * pairs[slot] + second
        pick = (key_group == group).astype(f32).astype(bf16)
        here = lax.dot_general(seen, pick, (((0,), (0,)), ((), ())), preferred_element_type=f32)
        allow = (key_group == group) | ((key_group < group) & (here > 0.5))
        bias[slot] = jnp.where(allow, 0.0, MASKED).reshape(PAIRS // CHUNK, PARTS, ROWS)
        row_max[slot] = jnp.full((8, ROWS), LOWEST, f32)
        acc[slot] = jnp.zeros((HD + 16, ROWS), f32)

    def sibling(i):
        return remote(buf.at[c, i], buf.at[c, i], ssib.at[i], rsib.at[i], p, sib)

    def ring(main):
        if main:
            mine = jnp.where(extra, 2, c)
            there_n, there_p = jnp.where(near_extra, 2, c), jnp.where(far_extra, 2, c)
            dev_n, dev_p = (yn * NZ + z, hd), (yp * NZ + z, hd)
            here, after, before, opposite = y, yn, yp, yo
            sems, to_next, to_prev = rmain, snext, sprev
        else:
            mine, there_n, there_p = c, c, c
            dev_n, dev_p = (p, 2 * xn + c), (p, 2 * xp + c)
            here, after, before, opposite = x, xn, xp, xo
            sems, to_next, to_prev = rextra, enext, eprev

        def arrive(i):
            remote(buf.at[mine, i], buf.at[mine, i], to_next.at[0], sems.at[i], *dev_n).wait_recv()

        def go_next(i, s):
            return remote(buf.at[mine, i], buf.at[there_n, i], to_next.at[s], sems.at[i], *dev_n)

        def go_prev(i, s):
            return remote(buf.at[mine, i], buf.at[there_p, i], to_prev.at[s], sems.at[i], *dev_p)

        def when_next(even, act):
            if main:
                pl.when(jnp.logical_or(jnp.logical_not(near_extra), even))(act)
            else:
                act()

        def when_prev(odd, act):
            if main:
                pl.when(jnp.logical_or(jnp.logical_not(far_extra), odd))(act)
            else:
                act()

        def across(i):
            if main:

                @unless(extra)
                def _():
                    sibling(i).start()
            else:
                sibling(i).start()

        def own(n):
            i = here * NZ + away(n)
            arrive(i)
            when_next(n % 2 == 0, lambda: go_next(i, n).start())
            when_prev(n % 2 == 1, lambda: go_prev(i, n).start())
            across(i)

        def forward(j):
            i = before * NZ + away(2 * j)
            arrive(i)
            when_next(False, lambda: go_next(i, 8 + j).start())
            across(i)
            i = after * NZ + away(2 * j + 1)
            arrive(i)
            when_prev(False, lambda: go_prev(i, 8 + j).start())
            across(i)

        def rest(j):
            for i in (before * NZ + away(2 * j + 1), after * NZ + away(2 * j)):
                arrive(i)
                across(i)

        def far_side(n):
            i = opposite * NZ + away(n)
            arrive(i)
            across(i)

        def close(n):
            when_next(n % 2 == 0, lambda: go_next(n, n).wait_send())
            when_prev(n % 2 == 1, lambda: go_prev(n, n).wait_send())

        def close_forward(j):
            when_next(False, lambda: go_next(j, 8 + j).wait_send())
            when_prev(False, lambda: go_prev(j, 8 + j).wait_send())

        return own, forward, rest, far_side, close, close_forward

    main_ring, extra_ring = ring(True), ring(False)

    def turns_of(step, length):
        def one(n, carry):
            if step == 0:
                pl.when(n + AHEAD < NZ)(lambda: issue(n + AHEAD))
            if step in (2, 3):
                unless(extra)(lambda: main_ring[step](n))
            else:
                main_ring[step](n)
            pl.when(extra)(lambda: extra_ring[step](n))
            return carry

        lax.fori_loop(0, length, one, 0)

    def from_sibling(quarter):
        def one(b, carry):
            i = quarter * NZ + b
            remote(buf.at[1 - c, i], buf.at[1 - c, i], ssib.at[i], rsib.at[i], p, sib).wait_recv()
            return carry

        lax.fori_loop(0, NZ, one, 0)

    ones = jnp.ones((16, KEYS), bf16)
    scale = math.log2(math.e) / math.sqrt(HD)

    def attend(quarter):
        ends = []
        total = 0
        for slot in range(SLOTS):
            total = total + jnp.clip((pairs[slot] + 1 - NZ * quarter + CHUNK - 1) // CHUNK, 0, PER_QUARTER)
            ends.append(total)

        def item(i):
            slot, base = 0, 0
            for s in range(SLOTS - 1):
                past = i >= ends[s]
                slot = slot + past.astype(jnp.int32)
                base = jnp.where(past, ends[s], base)
            return slot, quarter * PER_QUARTER + jnp.clip(i - base, 0, PER_QUARTER - 1), i < total

        def score(i, s):
            slot, chunk, _ = item(i)
            keys = buf[0, pl.ds(CHUNK * chunk, CHUNK)].reshape(KEYS, HD)
            s[...] = jnp.dot(keys, qbuf[slot], preferred_element_type=f32)

        def weigh(i, probs, keep):
            slot, chunk, _ = item(i)
            values = jnp.concatenate(
                [buf[1, CHUNK * chunk + b, g * TOK : (g + 1) * TOK, :] for b in range(CHUNK) for g in range(2)], axis=1
            )
            values = jnp.concatenate([values, ones], axis=0)
            acc[slot] = acc[slot] * keep[0:1] + jnp.dot(values, probs[...], preferred_element_type=f32)

        def soften(i, s, probs, keep):
            slot, chunk, valid = item(i)
            offset = bias[slot, chunk] + jnp.where(valid, 0.0, MASKED)
            old = row_max[slot, 0:1]
            new = old
            for g in range(PARTS):
                top = jnp.max(s[g * TOK : (g + 1) * TOK, :], axis=0, keepdims=True)
                new = jnp.maximum(new, top * scale + offset[g : g + 1])
            keep[...] = jnp.broadcast_to(jnp.exp2(old - new), (8, ROWS))
            row_max[slot] = jnp.broadcast_to(new, (8, ROWS))
            for g in range(PARTS):
                t = s[g * TOK : (g + 1) * TOK, :] * scale + (offset[g : g + 1] - new)
                probs[g * TOK : (g + 1) * TOK, :] = jnp.exp2(t).astype(bf16)

        score(0, s_a)
        p_b[...] = jnp.zeros_like(p_b)
        keep_b[...] = jnp.ones_like(keep_b)

        def two(n, carry):
            i = 2 * n
            weigh(jnp.maximum(i - 1, 0), p_b, keep_b)
            score(i + 1, s_b)
            soften(i, s_a, p_a, keep_a)
            weigh(i, p_a, keep_a)
            score(i + 2, s_a)
            soften(i + 1, s_b, p_b, keep_b)
            return carry

        turns = (total + 1) // 2
        lax.fori_loop(0, turns, two, 0)

        @pl.when(turns > 0)
        def _():
            weigh(2 * turns - 1, p_b, keep_b)

    pair_quarter = [pairs[slot] // NZ for slot in range(SLOTS)]

    def stage_of(quarter):
        stage = 0
        for n in range(1, 4):
            stage = jnp.where(order[n] == quarter, n, stage)
        return stage

    stages = [stage_of(quarter) for quarter in range(4)]
    upto = [stages[0]]
    for quarter in range(1, 4):
        upto.append(jnp.maximum(upto[-1], stages[quarter]))

    def pick_one(values, i):
        chosen = values[0]
        for n in range(1, len(values)):
            chosen = jnp.where(i == n, values[n], chosen)
        return chosen

    def o_args(slot, g):
        pd = pick_one(pairs, slot) - 1 + g
        dst = att.at[pl.ds((1 - g) * TOK, TOK), pl.ds(pl.multiple_of(head * HD, HD), HD)]
        return o_buf.at[slot, g], dst, osend.at[2 * slot + g], orecv.at[(1 - g) * HEADS + head], pd, home

    def finish(stage):
        def one(slot, carry):
            pair = pick_one(pairs, slot)

            @pl.when(jnp.logical_and(pair >= 0, pick_one(upto, pair // NZ) == stage))
            def _():
                mixed = acc[slot, :HD] / acc[slot, HD : HD + 1]
                o_buf[slot, 1] = mixed[:, TOK:].T.astype(bf16)
                put(*o_args(slot, 1))
                o_buf[slot, 0] = mixed[:, :TOK].T.astype(bf16)

                @pl.when(pair >= 1)
                def _():
                    put(*o_args(slot, 0))

            return carry

        lax.fori_loop(0, SLOTS, one, 0)

    turns_of(0, NZ)
    for h in range(HEADS):
        put(*q_args(h))
    turns_of(1, 4)
    from_sibling(order[0])
    for slot in range(SLOTS):

        @pl.when(pairs[slot] >= 0)
        def _():
            remote(qt.at[0], qbuf.at[slot], qsend.at[0], qrecv.at[slot], p, hd).wait_recv()

    attend(order[0])
    finish(0)
    turns_of(2, 4)
    from_sibling(order[1])
    attend(order[1])
    finish(1)
    from_sibling(order[2])
    attend(order[2])
    finish(2)
    turns_of(3, NZ)
    from_sibling(order[3])
    attend(order[3])
    finish(3)

    def o_arrive(g):
        for h in range(HEADS):
            dst = att.at[pl.ds(g * TOK, TOK), pl.ds(h * HD, HD)]
            remote(dst, dst, osend.at[0], orecv.at[g * HEADS + h], p, hd).wait_recv()

    turn = (xo, xn, xp, x)

    def half_rows(t):
        return slice(t * TOK, (t + 1) * TOK)

    def part(t, j, core):
        cols = pl.ds(pl.multiple_of((2 * turn[j] + core) * WIDTH, HD), WIDTH)
        return jnp.dot(att[half_rows(t), :], w[:, cols], preferred_element_type=f32)

    def over(t, j):
        return remote(s1.at[t, j], r1.at[t, j], send1.at[4 * t + j], recv1.at[4 * t + j], p, sib)

    def far_copy(t):
        return remote(far.at[t], far_in.at[t], fsend.at[t], frecv.at[t], p, 2 * (xn, xp)[t] + c)

    def near_copy(t, d):
        i = 2 * t + d
        return remote(near.at[t, d], near_in.at[t, d], nsend.at[i], nrecv.at[i], p, 2 * (xn, xp)[d] + c)

    def send_parts(t):
        for j in range(4):
            s1[t, j] = part(t, j, 1 - c).astype(bf16)
            over(t, j).start()

        def both(j):
            mine = part(t, j, c)
            over(t, j).wait_recv()
            return mine + r1[t, j].astype(f32)

        far[t] = both(0).astype(bf16)
        far_copy(t).start()
        through, direct = t, 1 - t
        near[t, direct] = both(1 + direct).astype(bf16)
        near_copy(t, direct).start()
        through_sum = both(1 + through)
        keep[half_rows(t), :] = both(3)
        far_copy(t).wait_recv()
        near[t, through] = (through_sum + far_in[t].astype(f32)).astype(bf16)
        near_copy(t, through).start()

    def all_parts(t):
        total = keep[half_rows(t), :]
        for d in (1 - t, t):
            near_copy(t, d).wait_recv()
            total = total + near_in[t, d].astype(f32)
        return total

    loads[6].wait()
    loads[7].wait()
    o_arrive(0)
    send_parts(0)

    @unless(last)
    def _():
        o_arrive(1)

    send_parts(1)
    out_ref[:TOK, :] = (hid[TOK:, :].astype(f32) + gate[pl.ds(levels[1], 1), :] * all_parts(0)).astype(bf16)
    summed = all_parts(1)

    @pl.when(last)
    def _():
        out_ref[TOK:, :] = inc[...]

    @unless(last)
    def _():
        for copy in shift:
            copy.wait_recv()
        out_ref[TOK:, :] = (hs[...].astype(f32) + gs[0:1, :] * summed).astype(bf16)

    @pl.when(p > 0)
    def _():
        for copy in shift:
            copy.wait_send()

    for h in range(HEADS):
        for k in range(2):
            put_done(*(main_args(h, k) if h < 4 else extra_args(k)))
        put_done(*q_args(h))
    turns_of(4, NZ)
    turns_of(5, 4)

    def sibling_done(i, carry):
        sibling(i).wait_send()
        return carry

    lax.fori_loop(0, PAIRS, sibling_done, 0)
    for slot in range(SLOTS):

        @pl.when(pairs[slot] >= 0)
        def _():
            put_done(*o_args(slot, 1))

        @pl.when(pairs[slot] >= 1)
        def _():
            put_done(*o_args(slot, 0))

    for t in range(2):
        for j in range(4):
            over(t, j).wait_send()
        far_copy(t).wait_send()
        for d in range(2):
            near_copy(t, d).wait_send()


def on_device(query_states, key_states, value_states, hidden, out_weight, gate_table, levels, visible, incoming):
    dma = pltpu.SemaphoreType.DMA
    vmem = pltpu.VMEM
    return pl.pallas_call(
        body,
        out_shape=jax.ShapeDtypeStruct((ROWS, WIDTH), bf16),
        in_specs=[ANY] * 6 + [pl.BlockSpec(memory_space=pltpu.SMEM)] + [ANY] * 2,
        out_specs=pl.BlockSpec(memory_space=pltpu.VMEM),
        scratch_shapes=[
            vmem((ROWS, WIDTH), bf16),
            vmem((ROWS, WIDTH), bf16),
            vmem((ROWS, WIDTH), bf16),
            vmem((ROWS, WIDTH), bf16),
            vmem((WIDTH, 8 * WIDTH), bf16),
            vmem((LEVELS, WIDTH), f32),
            vmem((64, 64), jnp.int32),
            vmem((TOK, WIDTH), bf16),
            vmem((3, PAIRS, ROWS, HD), bf16),
            vmem((SLOTS, HD, ROWS), bf16),
            vmem((HEADS, HD, ROWS), bf16),
            vmem((HEADS, ROWS, HD), bf16),
            vmem((SLOTS, PAIRS // CHUNK, PARTS, ROWS), f32),
            vmem((KEYS, ROWS), f32),
            vmem((KEYS, ROWS), f32),
            vmem((KEYS, ROWS), bf16),
            vmem((KEYS, ROWS), bf16),
            vmem((8, ROWS), f32),
            vmem((8, ROWS), f32),
            vmem((SLOTS, 8, ROWS), f32),
            vmem((SLOTS, HD + 16, ROWS), f32),
            vmem((SLOTS, 2, TOK, HD), bf16),
            vmem((ROWS, WIDTH), bf16),
            vmem((2, 4, TOK, WIDTH), bf16),
            vmem((2, 4, TOK, WIDTH), bf16),
            vmem((2, TOK, WIDTH), bf16),
            vmem((2, TOK, WIDTH), bf16),
            vmem((2, 2, TOK, WIDTH), bf16),
            vmem((2, 2, TOK, WIDTH), bf16),
            vmem((ROWS, WIDTH), f32),
            vmem((TOK, WIDTH), bf16),
            vmem((8, WIDTH), f32),
            vmem((8, WIDTH), f32),
            dma((8,)),
            dma((5,)),
            dma((5,)),
            dma((5,)),
            dma((SLOTS,)),
            dma((PAIRS,)),
            dma((PAIRS,)),
            dma((PAIRS,)),
            dma((12,)),
            dma((12,)),
            dma((12,)),
            dma((12,)),
            dma((PAIRS,)),
            dma((2 * SLOTS,)),
            dma((2 * HEADS,)),
            dma((8,)),
            dma((8,)),
            dma((2,)),
            dma((2,)),
            dma((4,)),
            dma((4,)),
            dma((2,)),
            dma((2,)),
        ],
        compiler_params=pltpu.CompilerParams(has_side_effects=True, collective_id=0, vmem_limit_bytes=56 << 20),
        name="block",
    )(query_states, key_states, value_states, hidden, out_weight, gate_table, levels, visible, incoming)


def solution(mesh):
    return jax.shard_map(
        on_device,
        mesh=mesh,
        in_specs=(
            P("group", "head"),
            P("group", "head"),
            P("group", "head"),
            P("group", "head"),
            P("head", None),
            P(None, "head"),
            P("group"),
            P(),
            P(None, "head"),
        ),
        out_specs=P("group", "head"),
        check_vma=False,
    )
```

```python
import math

import jax
import jax.numpy as jnp
from jax import lax
from jax.experimental import pallas as pl
from jax.experimental.pallas import tpu as pltpu
from jax.sharding import PartitionSpec as P

HD = 128
TOK = 128
ROWS = 2 * TOK
NY, NZ, NX = 4, 8, 4
PAIRS = NY * NZ
HEADS = 5
WIDTH = HEADS * HD
LEVELS = 1000
MAIN_TEAM, EXTRA_TEAM = 6, 8
SLOTS = 6
CHUNK = 4
KEYS = CHUNK * ROWS
PARTS = 2 * CHUNK
PER_QUARTER = NZ // CHUNK
AHEAD = 8
QUERIES_AT = 4
MASKED = -1e30
LOWEST = -1e20
MESH = pl.DeviceIdType.MESH
ANY = pl.BlockSpec(memory_space=pl.ANY)
bf16 = jnp.bfloat16
f32 = jnp.float32


def remote(src, dst, send, recv, p, hd):
    return pltpu.make_async_remote_copy(
        src_ref=src, dst_ref=dst, send_sem=send, recv_sem=recv, device_id=(p, hd), device_id_type=MESH
    )


def unless(cond):
    return pl.when(jnp.logical_not(cond))


def pair_of(slot, size, rank):
    pos = jnp.where(slot % 2 == 0, rank, size - 1 - rank)
    return PAIRS - 1 - (slot * size + pos)


def owner_of(pair, head, x, c):
    size = MAIN_TEAM if head < 4 else EXTRA_TEAM
    t = PAIRS - 1 - pair
    slot = t // size
    pos = t % size
    rank = jnp.where(slot % 2 == 0, pos, size - 1 - pos)
    chip = rank // 2
    if head < 4:
        return ((head + 1 + chip) % NY) * NZ + 4 * c + head, 2 * x + rank % 2, slot
    return x * NZ + x + 4 * c, 2 * chip + rank % 2, slot


def body(
    q_hbm, k_hbm, v_hbm, hid_hbm, w_hbm, gate_hbm, levels, vis_hbm, inc_hbm, out_ref,
    q_in, k_in, v_in, hid, w, gate, vis, inc, buf, qbuf, qt, vt, bias, s_a, s_b, p_a, p_b, keep_a, keep_b,
    row_max, acc, o_buf, att, s1, r1, far, far_in, near, near_in, keep, hs, gs, gs_out,
    lsem, qsend, ksend, vsend, qrecv, rmain, rextra, rsib, snext, sprev, enext, eprev, ssib,
    osend, orecv, send1, recv1, fsend, frecv, nsend, nrecv, hsend, hrecv
):
    p = lax.axis_index("group")
    hd = lax.axis_index("head")
    y, z, x, c = p // NZ, p % NZ, hd // 2, hd % 2
    sib = 2 * x + 1 - c
    half, col = z // 4, z % 4
    extra = y == col
    last = p == PAIRS - 1
    size = jnp.where(extra, EXTRA_TEAM, MAIN_TEAM)
    rank = jnp.where(extra, 2 * x + c, 2 * ((y - col - 1 + NY) % NY) + c)
    head = jnp.where(extra, 4, col)
    home = jnp.where(extra, 2 * col, 2 * x) + half
    pairs = [pair_of(slot, size, rank) for slot in range(SLOTS)]
    yn, yp, yo = (y + 1) % NY, (y + 3) % NY, (y + 2) % NY
    xn, xp, xo = (x + 1) % NX, (x + 3) % NX, (x + 2) % NX
    near_extra, far_extra = yn == col, yp == col
    order = [jnp.where(extra, a, b) for a, b in ((x, y), (xp, yp), (xn, yn), (xo, yo))]

    def is_me(pd, hdd):
        return jnp.logical_and(pd == p, hdd == hd)

    loads = [
        pltpu.make_async_copy(src, dst, lsem.at[i])
        for i, (src, dst) in enumerate(
            [(k_hbm, k_in), (v_hbm, v_in), (q_hbm, q_in), (hid_hbm, hid), (vis_hbm, vis), (gate_hbm, gate), (w_hbm, w), (inc_hbm, inc)]
        )
    ]
    for copy in loads:
        copy.start()

    barrier = pltpu.get_barrier_semaphore()

    def ready(pd, hdd):
        pl.semaphore_signal(barrier, inc=1, device_id=(pd, hdd), device_id_type=MESH)

    def ready_unless_me(pd, hdd):
        @unless(is_me(pd, hdd))
        def _():
            ready(pd, hdd)

    for dz in range(NZ):
        ready_unless_me(y * NZ + dz, 2 * x + half)
    ready(yn * NZ + z, hd)
    ready(yp * NZ + z, hd)
    ready(p, sib)
    ready(p, 2 * xn + c)
    ready(p, 2 * xp + c)

    @pl.when(extra)
    def _():
        for dz in range(NZ):
            ready_unless_me(x * NZ + dz, home)

    for slot in range(SLOTS):

        @pl.when(pairs[slot] >= 0)
        def _():
            ready_unless_me(pairs[slot], home)

    @unless(last)
    def _():
        ready(p + 1, hd)

    def count(flag):
        return flag.astype(jnp.int32)

    def others(pd, hdd):
        return 1 - count(is_me(pd, hdd))

    expected = 2 + 1 + 2 + count(p > 0)
    for k in range(2):
        for h in range(4):
            expected = expected + others(y * NZ + 4 * c + h, 2 * x + k)
        expected = expected + others(x * NZ + x + 4 * c, 2 * y + k)
    for h in range(HEADS):
        pd, hdd, _ = owner_of(p, h, x, c)
        expected = expected + others(pd, hdd)

    def put(src, dst, send, recv, pd, hdd):
        @pl.when(is_me(pd, hdd))
        def _():
            pltpu.make_async_copy(src, dst, recv).start()

        @unless(is_me(pd, hdd))
        def _():
            remote(src, dst, send, recv, pd, hdd).start()

    def put_done(src, dst, send, recv, pd, hdd):
        @unless(is_me(pd, hdd))
        def _():
            remote(src, dst, send, recv, pd, hdd).wait_send()

    def main_args(h, k):
        src = k_in.at[:, pl.ds(pl.multiple_of(h * HD, HD), HD)] if k == 0 else vt.at[h]
        send = ksend.at[h] if k == 0 else vsend.at[h]
        return src, buf.at[jnp.where(y == h, 2, k), p], send, rmain.at[p], y * NZ + 4 * c + h, 2 * x + k

    def extra_args(k):
        src = k_in.at[:, pl.ds(4 * HD, HD)] if k == 0 else vt.at[4]
        send = ksend.at[4] if k == 0 else vsend.at[4]
        return src, buf.at[k, p], send, rextra.at[p], x * NZ + x + 4 * c, 2 * y + k

    def q_args(h):
        pd, hdd, slot = owner_of(p, h, x, c)
        return qt.at[h], qbuf.at[slot], qsend.at[h], qrecv.at[slot], pd, hdd

    for i in range(2):
        loads[i].wait()
    for h in range(HEADS):
        for g in range(2):
            vt[h, g * TOK : (g + 1) * TOK, :] = v_in[g * TOK : (g + 1) * TOK, h * HD : (h + 1) * HD].T
    for slot in range(3, SLOTS):

        @pl.when(pairs[slot] < 0)
        def _():
            qbuf[slot] = jnp.zeros((HD, ROWS), bf16)

    @pl.when(last)
    def _():
        att[TOK:, :] = jnp.zeros((TOK, WIDTH), bf16)

    pl.semaphore_wait(barrier, expected)

    def away(n):
        return (z + jnp.where(n % 2 == 1, (n + 1) // 2, NZ - n // 2)) % NZ

    def issue(n):
        zd = away(n)

        @pl.when(zd // 4 == c)
        def _():
            for k in range(2):
                put(*main_args(zd % 4, k))

        @pl.when(zd == x + 4 * c)
        def _():
            for k in range(2):
                put(*extra_args(k))

    for n in range(AHEAD):
        issue(n)
    loads[2].wait()
    for h in range(HEADS):
        qt[h] = q_in[:, h * HD : (h + 1) * HD].T

    for i in range(3, 6):
        loads[i].wait()
    gs_out[...] = jnp.broadcast_to(gate[pl.ds(levels[0], 1), :], (8, WIDTH))
    shift = [
        remote(hid.at[pl.ds(0, TOK)], hs, hsend.at[0], hrecv.at[0], p - 1, hd),
        remote(gs_out, gs, hsend.at[1], hrecv.at[1], p - 1, hd),
    ]

    @pl.when(p > 0)
    def _():
        for copy in shift:
            copy.start()

    seen = (vis[...] == 1).astype(f32).astype(bf16)
    key_group = lax.broadcasted_iota(jnp.int32, (64, ROWS), 0)
    second = (lax.broadcasted_iota(jnp.int32, (64, ROWS), 1) >= TOK).astype(jnp.int32)
    for slot in range(SLOTS):
        group = 2 * pairs[slot] + second
        pick = (key_group == group).astype(f32).astype(bf16)
        here = lax.dot_general(seen, pick, (((0,), (0,)), ((), ())), preferred_element_type=f32)
        allow = (key_group == group) | ((key_group < group) & (here > 0.5))
        bias[slot] = jnp.where(allow, 0.0, MASKED).reshape(PAIRS // CHUNK, PARTS, ROWS)
        row_max[slot] = jnp.full((8, ROWS), LOWEST, f32)
        acc[slot] = jnp.zeros((HD + 16, ROWS), f32)

    def sibling(i):
        return remote(buf.at[c, i], buf.at[c, i], ssib.at[i], rsib.at[i], p, sib)

    def ring(main):
        if main:
            mine = jnp.where(extra, 2, c)
            there_n, there_p = jnp.where(near_extra, 2, c), jnp.where(far_extra, 2, c)
            dev_n, dev_p = (yn * NZ + z, hd), (yp * NZ + z, hd)
            here, after, before, opposite = y, yn, yp, yo
            sems, to_next, to_prev = rmain, snext, sprev
        else:
            mine, there_n, there_p = c, c, c
            dev_n, dev_p = (p, 2 * xn + c), (p, 2 * xp + c)
            here, after, before, opposite = x, xn, xp, xo
            sems, to_next, to_prev = rextra, enext, eprev

        def arrive(i):
            remote(buf.at[mine, i], buf.at[mine, i], to_next.at[0], sems.at[i], *dev_n).wait_recv()

        def go_next(i, s):
            return remote(buf.at[mine, i], buf.at[there_n, i], to_next.at[s], sems.at[i], *dev_n)

        def go_prev(i, s):
            return remote(buf.at[mine, i], buf.at[there_p, i], to_prev.at[s], sems.at[i], *dev_p)

        def when_next(even, act):
            if main:
                pl.when(jnp.logical_or(jnp.logical_not(near_extra), even))(act)
            else:
                act()

        def when_prev(odd, act):
            if main:
                pl.when(jnp.logical_or(jnp.logical_not(far_extra), odd))(act)
            else:
                act()

        def across(i):
            if main:

                @unless(extra)
                def _():
                    sibling(i).start()
            else:
                sibling(i).start()

        def own(n):
            i = here * NZ + away(n)
            arrive(i)
            when_next(n % 2 == 0, lambda: go_next(i, n).start())
            when_prev(n % 2 == 1, lambda: go_prev(i, n).start())
            across(i)

        def forward(j):
            i = before * NZ + away(2 * j)
            arrive(i)
            when_next(False, lambda: go_next(i, 8 + j).start())
            across(i)
            i = after * NZ + away(2 * j + 1)
            arrive(i)
            when_prev(False, lambda: go_prev(i, 8 + j).start())
            across(i)

        def rest(j):
            for i in (before * NZ + away(2 * j + 1), after * NZ + away(2 * j)):
                arrive(i)
                across(i)

        def far_side(n):
            i = opposite * NZ + away(n)
            arrive(i)
            across(i)

        def close(n):
            when_next(n % 2 == 0, lambda: go_next(n, n).wait_send())
            when_prev(n % 2 == 1, lambda: go_prev(n, n).wait_send())

        def close_forward(j):
            when_next(False, lambda: go_next(j, 8 + j).wait_send())
            when_prev(False, lambda: go_prev(j, 8 + j).wait_send())

        return own, forward, rest, far_side, close, close_forward

    main_ring, extra_ring = ring(True), ring(False)

    def send_queries():
        for h in range(HEADS):
            put(*q_args(h))

    def turns_of(step, length):
        def one(n, carry):
            if step == 0:
                pl.when(n == QUERIES_AT)(send_queries)
                pl.when(n + AHEAD < NZ)(lambda: issue(n + AHEAD))
            if step in (2, 3):
                unless(extra)(lambda: main_ring[step](n))
            else:
                main_ring[step](n)
            pl.when(extra)(lambda: extra_ring[step](n))
            return carry

        lax.fori_loop(0, length, one, 0)

    def from_sibling(quarter):
        def one(b, carry):
            i = quarter * NZ + b
            remote(buf.at[1 - c, i], buf.at[1 - c, i], ssib.at[i], rsib.at[i], p, sib).wait_recv()
            return carry

        lax.fori_loop(0, NZ, one, 0)

    ones = jnp.ones((16, KEYS), bf16)
    scale = math.log2(math.e) / math.sqrt(HD)

    def attend(quarter):
        ends = []
        total = 0
        for slot in range(SLOTS):
            total = total + jnp.clip((pairs[slot] + 1 - NZ * quarter + CHUNK - 1) // CHUNK, 0, PER_QUARTER)
            ends.append(total)

        def item(i):
            slot, base = 0, 0
            for s in range(SLOTS - 1):
                past = i >= ends[s]
                slot = slot + past.astype(jnp.int32)
                base = jnp.where(past, ends[s], base)
            return slot, quarter * PER_QUARTER + jnp.clip(i - base, 0, PER_QUARTER - 1), i < total

        def score(i, s):
            slot, chunk, _ = item(i)
            keys = buf[0, pl.ds(CHUNK * chunk, CHUNK)].reshape(KEYS, HD)
            s[...] = jnp.dot(keys, qbuf[slot], preferred_element_type=f32)

        def weigh(i, probs, keep):
            slot, chunk, _ = item(i)
            values = jnp.concatenate(
                [buf[1, CHUNK * chunk + b, g * TOK : (g + 1) * TOK, :] for b in range(CHUNK) for g in range(2)], axis=1
            )
            values = jnp.concatenate([values, ones], axis=0)
            acc[slot] = acc[slot] * keep[0:1] + jnp.dot(values, probs[...], preferred_element_type=f32)

        def soften(i, s, probs, keep):
            slot, chunk, valid = item(i)
            offset = bias[slot, chunk] + jnp.where(valid, 0.0, MASKED)
            old = row_max[slot, 0:1]
            new = old
            for g in range(PARTS):
                top = jnp.max(s[g * TOK : (g + 1) * TOK, :], axis=0, keepdims=True)
                new = jnp.maximum(new, top * scale + offset[g : g + 1])
            keep[...] = jnp.broadcast_to(jnp.exp2(old - new), (8, ROWS))
            row_max[slot] = jnp.broadcast_to(new, (8, ROWS))
            for g in range(PARTS):
                t = s[g * TOK : (g + 1) * TOK, :] * scale + (offset[g : g + 1] - new)
                probs[g * TOK : (g + 1) * TOK, :] = jnp.exp2(t).astype(bf16)

        score(0, s_a)
        p_b[...] = jnp.zeros_like(p_b)
        keep_b[...] = jnp.ones_like(keep_b)

        def two(n, carry):
            i = 2 * n
            weigh(jnp.maximum(i - 1, 0), p_b, keep_b)
            score(i + 1, s_b)
            soften(i, s_a, p_a, keep_a)
            weigh(i, p_a, keep_a)
            score(i + 2, s_a)
            soften(i + 1, s_b, p_b, keep_b)
            return carry

        turns = (total + 1) // 2
        lax.fori_loop(0, turns, two, 0)

        @pl.when(turns > 0)
        def _():
            weigh(2 * turns - 1, p_b, keep_b)

    pair_quarter = [pairs[slot] // NZ for slot in range(SLOTS)]

    def stage_of(quarter):
        stage = 0
        for n in range(1, 4):
            stage = jnp.where(order[n] == quarter, n, stage)
        return stage

    stages = [stage_of(quarter) for quarter in range(4)]
    upto = [stages[0]]
    for quarter in range(1, 4):
        upto.append(jnp.maximum(upto[-1], stages[quarter]))

    def pick_one(values, i):
        chosen = values[0]
        for n in range(1, len(values)):
            chosen = jnp.where(i == n, values[n], chosen)
        return chosen

    def o_args(slot, g):
        pd = pick_one(pairs, slot) - 1 + g
        dst = att.at[pl.ds((1 - g) * TOK, TOK), pl.ds(pl.multiple_of(head * HD, HD), HD)]
        return o_buf.at[slot, g], dst, osend.at[2 * slot + g], orecv.at[(1 - g) * HEADS + head], pd, home

    def mix(slot, g):
        cols = slice(g * TOK, (g + 1) * TOK)
        o_buf[slot, g] = (acc[slot, :HD, cols] / acc[slot, HD : HD + 1, cols]).T.astype(bf16)

    def finish(stage):
        def one(slot, carry):
            pair = pick_one(pairs, slot)

            @pl.when(jnp.logical_and(pair >= 0, pick_one(upto, pair // NZ) == stage))
            def _():
                mix(slot, 1)
                put(*o_args(slot, 1))

            return carry

        lax.fori_loop(0, SLOTS, one, 0)

    turns_of(0, NZ)
    turns_of(1, 4)
    from_sibling(order[0])
    for slot in range(SLOTS):

        @pl.when(pairs[slot] >= 0)
        def _():
            remote(qt.at[0], qbuf.at[slot], qsend.at[0], qrecv.at[slot], p, hd).wait_recv()

    attend(order[0])
    finish(0)
    turns_of(2, 4)
    from_sibling(order[1])
    attend(order[1])
    finish(1)
    from_sibling(order[2])
    turns_of(3, NZ)
    attend(order[2])
    finish(2)
    from_sibling(order[3])
    attend(order[3])
    finish(3)

    def second_half(slot, carry):
        @pl.when(pick_one(pairs, slot) >= 0)
        def _():
            mix(slot, 0)
            put_done(*o_args(slot, 1))

        @pl.when(pick_one(pairs, slot) >= 1)
        def _():
            put(*o_args(slot, 0))

        return carry

    lax.fori_loop(0, SLOTS, second_half, 0)

    def o_arrive(g):
        for h in range(HEADS):
            dst = att.at[pl.ds(g * TOK, TOK), pl.ds(h * HD, HD)]
            remote(dst, dst, osend.at[0], orecv.at[g * HEADS + h], p, hd).wait_recv()

    turn = (xo, xn, xp, x)

    def half_rows(t):
        return slice(t * TOK, (t + 1) * TOK)

    def part(t, j, core):
        cols = pl.ds(pl.multiple_of((2 * turn[j] + core) * WIDTH, HD), WIDTH)
        return jnp.dot(att[half_rows(t), :], w[:, cols], preferred_element_type=f32)

    def over(t, j):
        return remote(s1.at[t, j], r1.at[t, j], send1.at[4 * t + j], recv1.at[4 * t + j], p, sib)

    def far_copy(t):
        return remote(far.at[t], far_in.at[t], fsend.at[t], frecv.at[t], p, 2 * (xn, xp)[t] + c)

    def near_copy(t, d):
        i = 2 * t + d
        return remote(near.at[t, d], near_in.at[t, d], nsend.at[i], nrecv.at[i], p, 2 * (xn, xp)[d] + c)

    def send_parts(t):
        through, direct = t, 1 - t

        def for_sibling(j):
            s1[t, j] = part(t, j, 1 - c).astype(bf16)
            over(t, j).start()

        def both(j, mine):
            over(t, j).wait_recv()
            return mine + r1[t, j].astype(f32)

        for_sibling(0)
        for_sibling(1 + direct)
        far[t] = both(0, part(t, 0, c)).astype(bf16)
        far_copy(t).start()
        near[t, direct] = both(1 + direct, part(t, 1 + direct, c)).astype(bf16)
        near_copy(t, direct).start()
        for_sibling(1 + through)
        for_sibling(3)
        through_sum = both(1 + through, part(t, 1 + through, c))
        keep[half_rows(t), :] = both(3, part(t, 3, c))
        far_copy(t).wait_recv()
        near[t, through] = (through_sum + far_in[t].astype(f32)).astype(bf16)
        near_copy(t, through).start()

    def all_parts(t):
        total = keep[half_rows(t), :]
        for d in (1 - t, t):
            near_copy(t, d).wait_recv()
            total = total + near_in[t, d].astype(f32)
        return total

    loads[6].wait()
    loads[7].wait()
    o_arrive(0)
    send_parts(0)

    @unless(last)
    def _():
        o_arrive(1)

    send_parts(1)
    out_ref[:TOK, :] = (hid[TOK:, :].astype(f32) + gate[pl.ds(levels[1], 1), :] * all_parts(0)).astype(bf16)
    summed = all_parts(1)

    @pl.when(last)
    def _():
        out_ref[TOK:, :] = inc[...]

    @unless(last)
    def _():
        for copy in shift:
            copy.wait_recv()
        out_ref[TOK:, :] = (hs[...].astype(f32) + gs[0:1, :] * summed).astype(bf16)

    @pl.when(p > 0)
    def _():
        for copy in shift:
            copy.wait_send()

    for h in range(HEADS):
        for k in range(2):
            put_done(*(main_args(h, k) if h < 4 else extra_args(k)))
        put_done(*q_args(h))
    turns_of(4, NZ)
    turns_of(5, 4)

    def sibling_done(i, carry):
        sibling(i).wait_send()
        return carry

    lax.fori_loop(0, PAIRS, sibling_done, 0)
    for slot in range(SLOTS):

        @pl.when(pairs[slot] >= 1)
        def _():
            put_done(*o_args(slot, 0))

    for t in range(2):
        for j in range(4):
            over(t, j).wait_send()
        far_copy(t).wait_send()
        for d in range(2):
            near_copy(t, d).wait_send()


def on_device(query_states, key_states, value_states, hidden, out_weight, gate_table, levels, visible, incoming):
    dma = pltpu.SemaphoreType.DMA
    vmem = pltpu.VMEM
    return pl.pallas_call(
        body,
        out_shape=jax.ShapeDtypeStruct((ROWS, WIDTH), bf16),
        in_specs=[ANY] * 6 + [pl.BlockSpec(memory_space=pltpu.SMEM)] + [ANY] * 2,
        out_specs=pl.BlockSpec(memory_space=pltpu.VMEM),
        scratch_shapes=[
            vmem((ROWS, WIDTH), bf16),
            vmem((ROWS, WIDTH), bf16),
            vmem((ROWS, WIDTH), bf16),
            vmem((ROWS, WIDTH), bf16),
            vmem((WIDTH, 8 * WIDTH), bf16),
            vmem((LEVELS, WIDTH), f32),
            vmem((64, 64), jnp.int32),
            vmem((TOK, WIDTH), bf16),
            vmem((3, PAIRS, ROWS, HD), bf16),
            vmem((SLOTS, HD, ROWS), bf16),
            vmem((HEADS, HD, ROWS), bf16),
            vmem((HEADS, ROWS, HD), bf16),
            vmem((SLOTS, PAIRS // CHUNK, PARTS, ROWS), f32),
            vmem((KEYS, ROWS), f32),
            vmem((KEYS, ROWS), f32),
            vmem((KEYS, ROWS), bf16),
            vmem((KEYS, ROWS), bf16),
            vmem((8, ROWS), f32),
            vmem((8, ROWS), f32),
            vmem((SLOTS, 8, ROWS), f32),
            vmem((SLOTS, HD + 16, ROWS), f32),
            vmem((SLOTS, 2, TOK, HD), bf16),
            vmem((ROWS, WIDTH), bf16),
            vmem((2, 4, TOK, WIDTH), bf16),
            vmem((2, 4, TOK, WIDTH), bf16),
            vmem((2, TOK, WIDTH), bf16),
            vmem((2, TOK, WIDTH), bf16),
            vmem((2, 2, TOK, WIDTH), bf16),
            vmem((2, 2, TOK, WIDTH), bf16),
            vmem((ROWS, WIDTH), f32),
            vmem((TOK, WIDTH), bf16),
            vmem((8, WIDTH), f32),
            vmem((8, WIDTH), f32),
            dma((8,)),
            dma((5,)),
            dma((5,)),
            dma((5,)),
            dma((SLOTS,)),
            dma((PAIRS,)),
            dma((PAIRS,)),
            dma((PAIRS,)),
            dma((12,)),
            dma((12,)),
            dma((12,)),
            dma((12,)),
            dma((PAIRS,)),
            dma((2 * SLOTS,)),
            dma((2 * HEADS,)),
            dma((8,)),
            dma((8,)),
            dma((2,)),
            dma((2,)),
            dma((4,)),
            dma((4,)),
            dma((2,)),
            dma((2,)),
        ],
        compiler_params=pltpu.CompilerParams(has_side_effects=True, collective_id=0, vmem_limit_bytes=56 << 20),
        name="block",
    )(query_states, key_states, value_states, hidden, out_weight, gate_table, levels, visible, incoming)


def solution(mesh):
    return jax.shard_map(
        on_device,
        mesh=mesh,
        in_specs=(
            P("group", "head"),
            P("group", "head"),
            P("group", "head"),
            P("group", "head"),
            P("head", None),
            P(None, "head"),
            P("group"),
            P(),
            P(None, "head"),
        ),
        out_specs=P("group", "head"),
        check_vma=False,
    )
```

```python
import math

import jax
import jax.numpy as jnp
from jax import lax
from jax.experimental import pallas as pl
from jax.experimental.pallas import tpu as pltpu
from jax.sharding import PartitionSpec as P

HD = 128
TOK = 128
ROWS = 2 * TOK
NY, NZ, NX = 4, 8, 4
PAIRS = NY * NZ
HEADS = 5
WIDTH = HEADS * HD
LEVELS = 1000
MAIN_TEAM, EXTRA_TEAM = 6, 8
SLOTS = 6
CHUNK = 4
KEYS = CHUNK * ROWS
PARTS = 2 * CHUNK
PER_QUARTER = NZ // CHUNK
AHEAD = 8
QUERIES_AT = 4
PIECES = 4
MASKED = -1e30
LOWEST = -1e20
MESH = pl.DeviceIdType.MESH
ANY = pl.BlockSpec(memory_space=pl.ANY)
bf16 = jnp.bfloat16
f32 = jnp.float32


def remote(src, dst, send, recv, p, hd):
    return pltpu.make_async_remote_copy(
        src_ref=src, dst_ref=dst, send_sem=send, recv_sem=recv, device_id=(p, hd), device_id_type=MESH
    )


def unless(cond):
    return pl.when(jnp.logical_not(cond))


def pair_of(slot, size, rank):
    pos = jnp.where(slot % 2 == 0, rank, size - 1 - rank)
    return PAIRS - 1 - (slot * size + pos)


def owner_of(pair, head, x, c):
    size = MAIN_TEAM if head < 4 else EXTRA_TEAM
    t = PAIRS - 1 - pair
    slot = t // size
    pos = t % size
    rank = jnp.where(slot % 2 == 0, pos, size - 1 - pos)
    chip = rank // 2
    if head < 4:
        return ((head + 1 + chip) % NY) * NZ + 4 * c + head, 2 * x + rank % 2, slot
    return x * NZ + x + 4 * c, 2 * chip + rank % 2, slot


def body(
    q_hbm, k_hbm, v_hbm, hid_hbm, w_hbm, gate_hbm, levels, vis_hbm, inc_hbm, out_ref,
    q_in, k_in, v_in, hid, w, gate, vis, inc, buf, qbuf, qt, vt, bias, s_a, s_b, p_a, p_b, keep_a, keep_b,
    row_max, acc, o_buf, att, s1, r1, far, far_in, near, near_in, keep, hs, gs, gs_out,
    lsem, qsend, ksend, vsend, qrecv, rmain, rextra, rsib, snext, sprev, enext, eprev, ssib,
    osend, orecv, send1, recv1, fsend, frecv, nsend, nrecv, hsend, hrecv
):
    p = lax.axis_index("group")
    hd = lax.axis_index("head")
    y, z, x, c = p // NZ, p % NZ, hd // 2, hd % 2
    sib = 2 * x + 1 - c
    half, col = z // 4, z % 4
    extra = y == col
    last = p == PAIRS - 1
    size = jnp.where(extra, EXTRA_TEAM, MAIN_TEAM)
    rank = jnp.where(extra, 2 * x + c, 2 * ((y - col - 1 + NY) % NY) + c)
    head = jnp.where(extra, 4, col)
    home = jnp.where(extra, 2 * col, 2 * x) + half
    pairs = [pair_of(slot, size, rank) for slot in range(SLOTS)]
    yn, yp, yo = (y + 1) % NY, (y + 3) % NY, (y + 2) % NY
    xn, xp, xo = (x + 1) % NX, (x + 3) % NX, (x + 2) % NX
    near_extra, far_extra = yn == col, yp == col
    order = [jnp.where(extra, a, b) for a, b in ((x, y), (xp, yp), (xn, yn), (xo, yo))]

    def is_me(pd, hdd):
        return jnp.logical_and(pd == p, hdd == hd)

    loads = [
        pltpu.make_async_copy(src, dst, lsem.at[i])
        for i, (src, dst) in enumerate(
            [(k_hbm, k_in), (v_hbm, v_in), (q_hbm, q_in), (hid_hbm, hid), (vis_hbm, vis), (gate_hbm, gate), (w_hbm, w), (inc_hbm, inc)]
        )
    ]
    for copy in loads:
        copy.start()

    barrier = pltpu.get_barrier_semaphore()

    def ready(pd, hdd):
        pl.semaphore_signal(barrier, inc=1, device_id=(pd, hdd), device_id_type=MESH)

    def ready_unless_me(pd, hdd):
        @unless(is_me(pd, hdd))
        def _():
            ready(pd, hdd)

    for dz in range(NZ):
        ready_unless_me(y * NZ + dz, 2 * x + half)
    ready(yn * NZ + z, hd)
    ready(yp * NZ + z, hd)
    ready(p, sib)
    ready(p, 2 * xn + c)
    ready(p, 2 * xp + c)

    @pl.when(extra)
    def _():
        for dz in range(NZ):
            ready_unless_me(x * NZ + dz, home)

    for slot in range(SLOTS):

        @pl.when(pairs[slot] >= 0)
        def _():
            ready_unless_me(pairs[slot], home)

    @unless(last)
    def _():
        ready(p + 1, hd)

    def count(flag):
        return flag.astype(jnp.int32)

    def others(pd, hdd):
        return 1 - count(is_me(pd, hdd))

    expected = 2 + 1 + 2 + count(p > 0)
    for k in range(2):
        for h in range(4):
            expected = expected + others(y * NZ + 4 * c + h, 2 * x + k)
        expected = expected + others(x * NZ + x + 4 * c, 2 * y + k)
    for h in range(HEADS):
        pd, hdd, _ = owner_of(p, h, x, c)
        expected = expected + others(pd, hdd)

    def put(src, dst, send, recv, pd, hdd):
        @pl.when(is_me(pd, hdd))
        def _():
            pltpu.make_async_copy(src, dst, recv).start()

        @unless(is_me(pd, hdd))
        def _():
            remote(src, dst, send, recv, pd, hdd).start()

    def put_done(src, dst, send, recv, pd, hdd):
        @unless(is_me(pd, hdd))
        def _():
            remote(src, dst, send, recv, pd, hdd).wait_send()

    def main_args(h, k):
        src = k_in.at[:, pl.ds(pl.multiple_of(h * HD, HD), HD)] if k == 0 else vt.at[h]
        send = ksend.at[h] if k == 0 else vsend.at[h]
        return src, buf.at[jnp.where(y == h, 2, k), p], send, rmain.at[p], y * NZ + 4 * c + h, 2 * x + k

    def extra_args(k):
        src = k_in.at[:, pl.ds(4 * HD, HD)] if k == 0 else vt.at[4]
        send = ksend.at[4] if k == 0 else vsend.at[4]
        return src, buf.at[k, p], send, rextra.at[p], x * NZ + x + 4 * c, 2 * y + k

    def q_args(h):
        pd, hdd, slot = owner_of(p, h, x, c)
        return qt.at[h], qbuf.at[slot], qsend.at[h], qrecv.at[slot], pd, hdd

    for i in range(2):
        loads[i].wait()
    for h in range(HEADS):
        for g in range(2):
            vt[h, g * TOK : (g + 1) * TOK, :] = v_in[g * TOK : (g + 1) * TOK, h * HD : (h + 1) * HD].T
    for slot in range(3, SLOTS):

        @pl.when(pairs[slot] < 0)
        def _():
            qbuf[slot] = jnp.zeros((HD, ROWS), bf16)

    @pl.when(last)
    def _():
        att[TOK:, :] = jnp.zeros((TOK, WIDTH), bf16)

    pl.semaphore_wait(barrier, expected)

    def away(n):
        return (z + jnp.where(n % 2 == 1, (n + 1) // 2, NZ - n // 2)) % NZ

    def issue(n):
        zd = away(n)

        @pl.when(zd // 4 == c)
        def _():
            for k in range(2):
                put(*main_args(zd % 4, k))

        @pl.when(zd == x + 4 * c)
        def _():
            for k in range(2):
                put(*extra_args(k))

    for n in range(AHEAD):
        issue(n)
    loads[2].wait()
    for h in range(HEADS):
        qt[h] = q_in[:, h * HD : (h + 1) * HD].T

    for i in range(3, 6):
        loads[i].wait()
    gs_out[...] = jnp.broadcast_to(gate[pl.ds(levels[0], 1), :], (8, WIDTH))
    shift = [
        remote(hid.at[pl.ds(0, TOK)], hs, hsend.at[0], hrecv.at[0], p - 1, hd),
        remote(gs_out, gs, hsend.at[1], hrecv.at[1], p - 1, hd),
    ]

    @pl.when(p > 0)
    def _():
        for copy in shift:
            copy.start()

    seen = (vis[...] == 1).astype(f32).astype(bf16)
    key_group = lax.broadcasted_iota(jnp.int32, (64, ROWS), 0)
    second = (lax.broadcasted_iota(jnp.int32, (64, ROWS), 1) >= TOK).astype(jnp.int32)
    for slot in range(SLOTS):
        group = 2 * pairs[slot] + second
        pick = (key_group == group).astype(f32).astype(bf16)
        here = lax.dot_general(seen, pick, (((0,), (0,)), ((), ())), preferred_element_type=f32)
        allow = (key_group == group) | ((key_group < group) & (here > 0.5))
        bias[slot] = jnp.where(allow, 0.0, MASKED).reshape(PAIRS // CHUNK, PARTS, ROWS)
        row_max[slot] = jnp.full((8, ROWS), LOWEST, f32)
        acc[slot] = jnp.zeros((HD + 16, ROWS), f32)

    def sibling(i):
        return remote(buf.at[c, i], buf.at[c, i], ssib.at[i], rsib.at[i], p, sib)

    def ring(main):
        if main:
            mine = jnp.where(extra, 2, c)
            there_n, there_p = jnp.where(near_extra, 2, c), jnp.where(far_extra, 2, c)
            dev_n, dev_p = (yn * NZ + z, hd), (yp * NZ + z, hd)
            here, after, before, opposite = y, yn, yp, yo
            sems, to_next, to_prev = rmain, snext, sprev
        else:
            mine, there_n, there_p = c, c, c
            dev_n, dev_p = (p, 2 * xn + c), (p, 2 * xp + c)
            here, after, before, opposite = x, xn, xp, xo
            sems, to_next, to_prev = rextra, enext, eprev

        def arrive(i):
            remote(buf.at[mine, i], buf.at[mine, i], to_next.at[0], sems.at[i], *dev_n).wait_recv()

        def go_next(i, s):
            return remote(buf.at[mine, i], buf.at[there_n, i], to_next.at[s], sems.at[i], *dev_n)

        def go_prev(i, s):
            return remote(buf.at[mine, i], buf.at[there_p, i], to_prev.at[s], sems.at[i], *dev_p)

        def when_next(even, act):
            if main:
                pl.when(jnp.logical_or(jnp.logical_not(near_extra), even))(act)
            else:
                act()

        def when_prev(odd, act):
            if main:
                pl.when(jnp.logical_or(jnp.logical_not(far_extra), odd))(act)
            else:
                act()

        def across(i):
            if main:

                @unless(extra)
                def _():
                    sibling(i).start()
            else:
                sibling(i).start()

        def own(n):
            i = here * NZ + away(n)
            arrive(i)
            when_next(n % 2 == 0, lambda: go_next(i, n).start())
            when_prev(n % 2 == 1, lambda: go_prev(i, n).start())
            across(i)

        def forward(j):
            i = before * NZ + away(2 * j)
            arrive(i)
            when_next(False, lambda: go_next(i, 8 + j).start())
            across(i)
            i = after * NZ + away(2 * j + 1)
            arrive(i)
            when_prev(False, lambda: go_prev(i, 8 + j).start())
            across(i)

        def rest(j):
            for i in (before * NZ + away(2 * j + 1), after * NZ + away(2 * j)):
                arrive(i)
                across(i)

        def far_side(n):
            i = opposite * NZ + away(n)
            arrive(i)
            across(i)

        def close(n):
            when_next(n % 2 == 0, lambda: go_next(n, n).wait_send())
            when_prev(n % 2 == 1, lambda: go_prev(n, n).wait_send())

        def close_forward(j):
            when_next(False, lambda: go_next(j, 8 + j).wait_send())
            when_prev(False, lambda: go_prev(j, 8 + j).wait_send())

        return own, forward, rest, far_side, close, close_forward

    main_ring, extra_ring = ring(True), ring(False)

    def send_queries():
        for h in range(HEADS):
            put(*q_args(h))

    def turns_of(step, length):
        def one(n, carry):
            if step == 0:
                pl.when(n == QUERIES_AT)(send_queries)
                pl.when(n + AHEAD < NZ)(lambda: issue(n + AHEAD))
            if step in (2, 3):
                unless(extra)(lambda: main_ring[step](n))
            else:
                main_ring[step](n)
            pl.when(extra)(lambda: extra_ring[step](n))
            return carry

        lax.fori_loop(0, length, one, 0)

    def from_sibling(quarter):
        def one(b, carry):
            i = quarter * NZ + b
            remote(buf.at[1 - c, i], buf.at[1 - c, i], ssib.at[i], rsib.at[i], p, sib).wait_recv()
            return carry

        lax.fori_loop(0, NZ, one, 0)

    ones = jnp.ones((16, KEYS), bf16)
    scale = math.log2(math.e) / math.sqrt(HD)

    def attend(quarter):
        ends = []
        total = 0
        for slot in range(SLOTS):
            total = total + jnp.clip((pairs[slot] + 1 - NZ * quarter + CHUNK - 1) // CHUNK, 0, PER_QUARTER)
            ends.append(total)

        def item(i):
            slot, base = 0, 0
            for s in range(SLOTS - 1):
                past = i >= ends[s]
                slot = slot + past.astype(jnp.int32)
                base = jnp.where(past, ends[s], base)
            return slot, quarter * PER_QUARTER + jnp.clip(i - base, 0, PER_QUARTER - 1), i < total

        def score(i, s):
            slot, chunk, _ = item(i)
            keys = buf[0, pl.ds(CHUNK * chunk, CHUNK)].reshape(KEYS, HD)
            s[...] = jnp.dot(keys, qbuf[slot], preferred_element_type=f32)

        def weigh(i, probs, keep):
            slot, chunk, _ = item(i)
            values = jnp.concatenate(
                [buf[1, CHUNK * chunk + b, g * TOK : (g + 1) * TOK, :] for b in range(CHUNK) for g in range(2)], axis=1
            )
            values = jnp.concatenate([values, ones], axis=0)
            acc[slot] = acc[slot] * keep[0:1] + jnp.dot(values, probs[...], preferred_element_type=f32)

        def soften(i, s, probs, keep):
            slot, chunk, valid = item(i)
            offset = bias[slot, chunk] + jnp.where(valid, 0.0, MASKED)
            old = row_max[slot, 0:1]
            new = old
            for g in range(PARTS):
                top = jnp.max(s[g * TOK : (g + 1) * TOK, :], axis=0, keepdims=True)
                new = jnp.maximum(new, top * scale + offset[g : g + 1])
            keep[...] = jnp.broadcast_to(jnp.exp2(old - new), (8, ROWS))
            row_max[slot] = jnp.broadcast_to(new, (8, ROWS))
            for g in range(PARTS):
                t = s[g * TOK : (g + 1) * TOK, :] * scale + (offset[g : g + 1] - new)
                probs[g * TOK : (g + 1) * TOK, :] = jnp.exp2(t).astype(bf16)

        score(0, s_a)
        p_b[...] = jnp.zeros_like(p_b)
        keep_b[...] = jnp.ones_like(keep_b)

        def two(n, carry):
            i = 2 * n
            weigh(jnp.maximum(i - 1, 0), p_b, keep_b)
            score(i + 1, s_b)
            soften(i, s_a, p_a, keep_a)
            weigh(i, p_a, keep_a)
            score(i + 2, s_a)
            soften(i + 1, s_b, p_b, keep_b)
            return carry

        turns = (total + 1) // 2
        lax.fori_loop(0, turns, two, 0)

        @pl.when(turns > 0)
        def _():
            weigh(2 * turns - 1, p_b, keep_b)

    pair_quarter = [pairs[slot] // NZ for slot in range(SLOTS)]

    def stage_of(quarter):
        stage = 0
        for n in range(1, 4):
            stage = jnp.where(order[n] == quarter, n, stage)
        return stage

    stages = [stage_of(quarter) for quarter in range(4)]
    upto = [stages[0]]
    for quarter in range(1, 4):
        upto.append(jnp.maximum(upto[-1], stages[quarter]))

    def pick_one(values, i):
        chosen = values[0]
        for n in range(1, len(values)):
            chosen = jnp.where(i == n, values[n], chosen)
        return chosen

    def o_args(slot, g):
        pd = pick_one(pairs, slot) - 1 + g
        dst = att.at[pl.ds((1 - g) * TOK, TOK), pl.ds(pl.multiple_of(head * HD, HD), HD)]
        return o_buf.at[slot, g], dst, osend.at[2 * slot + g], orecv.at[(1 - g) * HEADS + head], pd, home

    def mix(slot, g):
        cols = slice(g * TOK, (g + 1) * TOK)
        o_buf[slot, g] = (acc[slot, :HD, cols] / acc[slot, HD : HD + 1, cols]).T.astype(bf16)

    def finish(stage):
        def one(slot, carry):
            pair = pick_one(pairs, slot)

            @pl.when(jnp.logical_and(pair >= 0, pick_one(upto, pair // NZ) == stage))
            def _():
                mix(slot, 1)
                put(*o_args(slot, 1))

            return carry

        lax.fori_loop(0, SLOTS, one, 0)

    turns_of(0, NZ)
    turns_of(1, 4)
    from_sibling(order[0])
    for slot in range(SLOTS):

        @pl.when(pairs[slot] >= 0)
        def _():
            remote(qt.at[0], qbuf.at[slot], qsend.at[0], qrecv.at[slot], p, hd).wait_recv()

    attend(order[0])
    finish(0)
    turns_of(2, 4)
    from_sibling(order[1])
    attend(order[1])
    finish(1)
    from_sibling(order[2])
    turns_of(3, NZ)
    attend(order[2])
    finish(2)
    from_sibling(order[3])
    attend(order[3])
    finish(3)

    def second_half(slot, carry):
        @pl.when(pick_one(pairs, slot) >= 0)
        def _():
            mix(slot, 0)
            put_done(*o_args(slot, 1))

        @pl.when(pick_one(pairs, slot) >= 1)
        def _():
            put(*o_args(slot, 0))

        return carry

    lax.fori_loop(0, SLOTS, second_half, 0)

    def o_arrive(g):
        for h in range(HEADS):
            dst = att.at[pl.ds(g * TOK, TOK), pl.ds(h * HD, HD)]
            remote(dst, dst, osend.at[0], orecv.at[g * HEADS + h], p, hd).wait_recv()

    turn = (xo, xn, xp, x)

    def half_rows(t):
        return slice(t * TOK, (t + 1) * TOK)

    def part(t, j, core):
        cols = pl.ds(pl.multiple_of((2 * turn[j] + core) * WIDTH, HD), WIDTH)
        return jnp.dot(att[half_rows(t), :], w[:, cols], preferred_element_type=f32)

    def over(t, j):
        return remote(s1.at[t, j], r1.at[t, j], send1.at[4 * t + j], recv1.at[4 * t + j], p, sib)

    piece = TOK // PIECES

    def piece_rows(u):
        return slice(u * piece, (u + 1) * piece)

    def far_copy(t, u):
        i = PIECES * t + u
        rows = pl.ds(u * piece, piece)
        return remote(far.at[t, rows], far_in.at[t, rows], fsend.at[i], frecv.at[i], p, 2 * (xn, xp)[t] + c)

    def near_copy(t, d, u):
        i = PIECES * (2 * t + d) + u
        rows = pl.ds(u * piece, piece)
        return remote(near.at[t, d, rows], near_in.at[t, d, rows], nsend.at[i], nrecv.at[i], p, 2 * (xn, xp)[d] + c)

    def send_parts(t):
        through, direct = t, 1 - t

        def for_sibling(j):
            s1[t, j] = part(t, j, 1 - c).astype(bf16)
            over(t, j).start()

        def both(j, mine):
            over(t, j).wait_recv()
            return mine + r1[t, j].astype(f32)

        for_sibling(0)
        for_sibling(1 + direct)
        far[t] = both(0, part(t, 0, c)).astype(bf16)
        for u in range(PIECES):
            far_copy(t, u).start()
        near[t, direct] = both(1 + direct, part(t, 1 + direct, c)).astype(bf16)
        for u in range(PIECES):
            near_copy(t, direct, u).start()
        for_sibling(1 + through)
        for_sibling(3)
        through_sum = both(1 + through, part(t, 1 + through, c))
        keep[half_rows(t), :] = both(3, part(t, 3, c))
        for u in range(PIECES):
            rows = piece_rows(u)
            far_copy(t, u).wait_recv()
            near[t, through, rows] = (through_sum[rows] + far_in[t, rows].astype(f32)).astype(bf16)
            near_copy(t, through, u).start()

    def all_parts(t):
        total = keep[half_rows(t), :]
        for d in (1 - t, t):
            for u in range(PIECES):
                near_copy(t, d, u).wait_recv()
            total = total + near_in[t, d].astype(f32)
        return total

    loads[6].wait()
    loads[7].wait()
    o_arrive(0)
    send_parts(0)

    @unless(last)
    def _():
        o_arrive(1)

    send_parts(1)
    out_ref[:TOK, :] = (hid[TOK:, :].astype(f32) + gate[pl.ds(levels[1], 1), :] * all_parts(0)).astype(bf16)
    summed = all_parts(1)

    @pl.when(last)
    def _():
        out_ref[TOK:, :] = inc[...]

    @unless(last)
    def _():
        for copy in shift:
            copy.wait_recv()
        out_ref[TOK:, :] = (hs[...].astype(f32) + gs[0:1, :] * summed).astype(bf16)

    @pl.when(p > 0)
    def _():
        for copy in shift:
            copy.wait_send()

    for h in range(HEADS):
        for k in range(2):
            put_done(*(main_args(h, k) if h < 4 else extra_args(k)))
        put_done(*q_args(h))
    turns_of(4, NZ)
    turns_of(5, 4)

    def sibling_done(i, carry):
        sibling(i).wait_send()
        return carry

    lax.fori_loop(0, PAIRS, sibling_done, 0)
    for slot in range(SLOTS):

        @pl.when(pairs[slot] >= 1)
        def _():
            put_done(*o_args(slot, 0))

    for t in range(2):
        for j in range(4):
            over(t, j).wait_send()
        for u in range(PIECES):
            far_copy(t, u).wait_send()
            for d in range(2):
                near_copy(t, d, u).wait_send()


def on_device(query_states, key_states, value_states, hidden, out_weight, gate_table, levels, visible, incoming):
    dma = pltpu.SemaphoreType.DMA
    vmem = pltpu.VMEM
    return pl.pallas_call(
        body,
        out_shape=jax.ShapeDtypeStruct((ROWS, WIDTH), bf16),
        in_specs=[ANY] * 6 + [pl.BlockSpec(memory_space=pltpu.SMEM)] + [ANY] * 2,
        out_specs=pl.BlockSpec(memory_space=pltpu.VMEM),
        scratch_shapes=[
            vmem((ROWS, WIDTH), bf16),
            vmem((ROWS, WIDTH), bf16),
            vmem((ROWS, WIDTH), bf16),
            vmem((ROWS, WIDTH), bf16),
            vmem((WIDTH, 8 * WIDTH), bf16),
            vmem((LEVELS, WIDTH), f32),
            vmem((64, 64), jnp.int32),
            vmem((TOK, WIDTH), bf16),
            vmem((3, PAIRS, ROWS, HD), bf16),
            vmem((SLOTS, HD, ROWS), bf16),
            vmem((HEADS, HD, ROWS), bf16),
            vmem((HEADS, ROWS, HD), bf16),
            vmem((SLOTS, PAIRS // CHUNK, PARTS, ROWS), f32),
            vmem((KEYS, ROWS), f32),
            vmem((KEYS, ROWS), f32),
            vmem((KEYS, ROWS), bf16),
            vmem((KEYS, ROWS), bf16),
            vmem((8, ROWS), f32),
            vmem((8, ROWS), f32),
            vmem((SLOTS, 8, ROWS), f32),
            vmem((SLOTS, HD + 16, ROWS), f32),
            vmem((SLOTS, 2, TOK, HD), bf16),
            vmem((ROWS, WIDTH), bf16),
            vmem((2, 4, TOK, WIDTH), bf16),
            vmem((2, 4, TOK, WIDTH), bf16),
            vmem((2, TOK, WIDTH), bf16),
            vmem((2, TOK, WIDTH), bf16),
            vmem((2, 2, TOK, WIDTH), bf16),
            vmem((2, 2, TOK, WIDTH), bf16),
            vmem((ROWS, WIDTH), f32),
            vmem((TOK, WIDTH), bf16),
            vmem((8, WIDTH), f32),
            vmem((8, WIDTH), f32),
            dma((8,)),
            dma((5,)),
            dma((5,)),
            dma((5,)),
            dma((SLOTS,)),
            dma((PAIRS,)),
            dma((PAIRS,)),
            dma((PAIRS,)),
            dma((12,)),
            dma((12,)),
            dma((12,)),
            dma((12,)),
            dma((PAIRS,)),
            dma((2 * SLOTS,)),
            dma((2 * HEADS,)),
            dma((8,)),
            dma((8,)),
            dma((2 * PIECES,)),
            dma((2 * PIECES,)),
            dma((4 * PIECES,)),
            dma((4 * PIECES,)),
            dma((2,)),
            dma((2,)),
        ],
        compiler_params=pltpu.CompilerParams(has_side_effects=True, collective_id=0, vmem_limit_bytes=56 << 20),
        name="block",
    )(query_states, key_states, value_states, hidden, out_weight, gate_table, levels, visible, incoming)


def solution(mesh):
    return jax.shard_map(
        on_device,
        mesh=mesh,
        in_specs=(
            P("group", "head"),
            P("group", "head"),
            P("group", "head"),
            P("group", "head"),
            P("head", None),
            P(None, "head"),
            P("group"),
            P(),
            P(None, "head"),
        ),
        out_specs=P("group", "head"),
        check_vma=False,
    )
```

```python
import math

import jax
import jax.numpy as jnp
from jax import lax
from jax.experimental import pallas as pl
from jax.experimental.pallas import tpu as pltpu
from jax.sharding import PartitionSpec as P

HD = 128
TOK = 128
ROWS = 2 * TOK
NY, NZ, NX = 4, 8, 4
PAIRS = NY * NZ
HEADS = 5
WIDTH = HEADS * HD
LEVELS = 1000
MAIN_TEAM, EXTRA_TEAM = 6, 8
SLOTS = 6
CHUNK = 4
KEYS = CHUNK * ROWS
PARTS = 2 * CHUNK
PER_QUARTER = NZ // CHUNK
AHEAD = 8
QUERIES_AT = 4
PIECES = 4
MASKED = -1e30
LOWEST = -1e20
MESH = pl.DeviceIdType.MESH
ANY = pl.BlockSpec(memory_space=pl.ANY)
bf16 = jnp.bfloat16
f32 = jnp.float32


def remote(src, dst, send, recv, p, hd):
    return pltpu.make_async_remote_copy(
        src_ref=src, dst_ref=dst, send_sem=send, recv_sem=recv, device_id=(p, hd), device_id_type=MESH
    )


def unless(cond):
    return pl.when(jnp.logical_not(cond))


def pair_of(slot, size, rank):
    pos = jnp.where(slot % 2 == 0, rank, size - 1 - rank)
    return PAIRS - 1 - (slot * size + pos)


def owner_of(pair, head, x, c):
    size = MAIN_TEAM if head < 4 else EXTRA_TEAM
    t = PAIRS - 1 - pair
    slot = t // size
    pos = t % size
    rank = jnp.where(slot % 2 == 0, pos, size - 1 - pos)
    chip = rank // 2
    if head < 4:
        return ((head + 1 + chip) % NY) * NZ + 4 * c + head, 2 * x + rank % 2, slot
    return x * NZ + x + 4 * c, 2 * chip + rank % 2, slot


def body(
    q_hbm, k_hbm, v_hbm, hid_hbm, w_hbm, gate_hbm, levels, vis_hbm, inc_hbm, out_ref,
    q_in, k_in, v_in, hid, w, gate, vis, inc, buf, qbuf, qt, vt, bias, s_a, s_b, p_a, p_b, keep_a, keep_b,
    row_max, acc, o_buf, att, s1, r1, far, far_in, near, near_in, keep, hs, gs, gs_out,
    lsem, qsend, ksend, vsend, qrecv, rmain, rextra, rsib, snext, sprev, enext, eprev, ssib,
    osend, orecv, send1, recv1, fsend, frecv, nsend, nrecv, hsend, hrecv
):
    p = lax.axis_index("group")
    hd = lax.axis_index("head")
    y, z, x, c = p // NZ, p % NZ, hd // 2, hd % 2
    sib = 2 * x + 1 - c
    half, col = z // 4, z % 4
    extra = y == col
    last = p == PAIRS - 1
    size = jnp.where(extra, EXTRA_TEAM, MAIN_TEAM)
    rank = jnp.where(extra, 2 * x + c, 2 * ((y - col - 1 + NY) % NY) + c)
    head = jnp.where(extra, 4, col)
    home = jnp.where(extra, 2 * col, 2 * x) + half
    pairs = [pair_of(slot, size, rank) for slot in range(SLOTS)]
    yn, yp, yo = (y + 1) % NY, (y + 3) % NY, (y + 2) % NY
    xn, xp, xo = (x + 1) % NX, (x + 3) % NX, (x + 2) % NX
    near_extra, far_extra = yn == col, yp == col
    order = [jnp.where(extra, a, b) for a, b in ((x, y), (xp, yp), (xn, yn), (xo, yo))]

    def is_me(pd, hdd):
        return jnp.logical_and(pd == p, hdd == hd)

    loads = [
        pltpu.make_async_copy(src, dst, lsem.at[i])
        for i, (src, dst) in enumerate(
            [(k_hbm, k_in), (v_hbm, v_in), (q_hbm, q_in), (hid_hbm, hid), (vis_hbm, vis), (gate_hbm, gate), (w_hbm, w), (inc_hbm, inc)]
        )
    ]
    for copy in loads:
        copy.start()

    barrier = pltpu.get_barrier_semaphore()

    def ready(pd, hdd):
        pl.semaphore_signal(barrier, inc=1, device_id=(pd, hdd), device_id_type=MESH)

    def ready_unless_me(pd, hdd):
        @unless(is_me(pd, hdd))
        def _():
            ready(pd, hdd)

    for dz in range(NZ):
        ready_unless_me(y * NZ + dz, 2 * x + half)
    ready(yn * NZ + z, hd)
    ready(yp * NZ + z, hd)
    ready(p, sib)
    ready(p, 2 * xn + c)
    ready(p, 2 * xp + c)

    @pl.when(extra)
    def _():
        for dz in range(NZ):
            ready_unless_me(x * NZ + dz, home)

    for slot in range(SLOTS):

        @pl.when(pairs[slot] >= 0)
        def _():
            ready_unless_me(pairs[slot], home)

    @unless(last)
    def _():
        ready(p + 1, hd)

    def count(flag):
        return flag.astype(jnp.int32)

    def others(pd, hdd):
        return 1 - count(is_me(pd, hdd))

    expected = 2 + 1 + 2 + count(p > 0)
    for k in range(2):
        for h in range(4):
            expected = expected + others(y * NZ + 4 * c + h, 2 * x + k)
        expected = expected + others(x * NZ + x + 4 * c, 2 * y + k)
    for h in range(HEADS):
        pd, hdd, _ = owner_of(p, h, x, c)
        expected = expected + others(pd, hdd)

    def put(src, dst, send, recv, pd, hdd):
        @pl.when(is_me(pd, hdd))
        def _():
            pltpu.make_async_copy(src, dst, recv).start()

        @unless(is_me(pd, hdd))
        def _():
            remote(src, dst, send, recv, pd, hdd).start()

    def put_done(src, dst, send, recv, pd, hdd):
        @unless(is_me(pd, hdd))
        def _():
            remote(src, dst, send, recv, pd, hdd).wait_send()

    def main_args(h, k):
        src = k_in.at[:, pl.ds(pl.multiple_of(h * HD, HD), HD)] if k == 0 else vt.at[h]
        send = ksend.at[h] if k == 0 else vsend.at[h]
        return src, buf.at[jnp.where(y == h, 2, k), p], send, rmain.at[p], y * NZ + 4 * c + h, 2 * x + k

    def extra_args(k):
        src = k_in.at[:, pl.ds(4 * HD, HD)] if k == 0 else vt.at[4]
        send = ksend.at[4] if k == 0 else vsend.at[4]
        return src, buf.at[k, p], send, rextra.at[p], x * NZ + x + 4 * c, 2 * y + k

    def q_args(h):
        pd, hdd, slot = owner_of(p, h, x, c)
        return qt.at[h], qbuf.at[slot], qsend.at[h], qrecv.at[slot], pd, hdd

    for i in range(2):
        loads[i].wait()
    for h in range(HEADS):
        for g in range(2):
            vt[h, g * TOK : (g + 1) * TOK, :] = v_in[g * TOK : (g + 1) * TOK, h * HD : (h + 1) * HD].T
    for slot in range(3, SLOTS):

        @pl.when(pairs[slot] < 0)
        def _():
            qbuf[slot] = jnp.zeros((HD, ROWS), bf16)

    @pl.when(last)
    def _():
        att[TOK:, :] = jnp.zeros((TOK, WIDTH), bf16)

    pl.semaphore_wait(barrier, expected)

    def away(n):
        return (z + jnp.where(n % 2 == 1, (n + 1) // 2, NZ - n // 2)) % NZ

    def issue(n):
        zd = away(n)

        @pl.when(zd // 4 == c)
        def _():
            for k in range(2):
                put(*main_args(zd % 4, k))

        @pl.when(zd == x + 4 * c)
        def _():
            for k in range(2):
                put(*extra_args(k))

    for n in range(AHEAD):
        issue(n)
    loads[2].wait()
    for h in range(HEADS):
        qt[h] = q_in[:, h * HD : (h + 1) * HD].T

    for i in range(3, 6):
        loads[i].wait()
    gs_out[...] = jnp.broadcast_to(gate[pl.ds(levels[0], 1), :], (8, WIDTH))
    shift = [
        remote(hid.at[pl.ds(0, TOK)], hs, hsend.at[0], hrecv.at[0], p - 1, hd),
        remote(gs_out, gs, hsend.at[1], hrecv.at[1], p - 1, hd),
    ]

    @pl.when(p > 0)
    def _():
        for copy in shift:
            copy.start()

    seen = (vis[...] == 1).astype(f32).astype(bf16)
    key_group = lax.broadcasted_iota(jnp.int32, (64, ROWS), 0)
    second = (lax.broadcasted_iota(jnp.int32, (64, ROWS), 1) >= TOK).astype(jnp.int32)
    for slot in range(SLOTS):
        group = 2 * pairs[slot] + second
        pick = (key_group == group).astype(f32).astype(bf16)
        here = lax.dot_general(seen, pick, (((0,), (0,)), ((), ())), preferred_element_type=f32)
        allow = (key_group == group) | ((key_group < group) & (here > 0.5))
        bias[slot] = jnp.where(allow, 0.0, MASKED).reshape(PAIRS // CHUNK, PARTS, ROWS)
        row_max[slot] = jnp.full((8, ROWS), LOWEST, f32)
        acc[slot] = jnp.zeros((HD + 16, ROWS), f32)

    def sibling(i):
        return remote(buf.at[c, i], buf.at[c, i], ssib.at[i], rsib.at[i], p, sib)

    def ring(main):
        if main:
            mine = jnp.where(extra, 2, c)
            there_n, there_p = jnp.where(near_extra, 2, c), jnp.where(far_extra, 2, c)
            dev_n, dev_p = (yn * NZ + z, hd), (yp * NZ + z, hd)
            here, after, before, opposite = y, yn, yp, yo
            sems, to_next, to_prev = rmain, snext, sprev
        else:
            mine, there_n, there_p = c, c, c
            dev_n, dev_p = (p, 2 * xn + c), (p, 2 * xp + c)
            here, after, before, opposite = x, xn, xp, xo
            sems, to_next, to_prev = rextra, enext, eprev

        def arrive(i):
            remote(buf.at[mine, i], buf.at[mine, i], to_next.at[0], sems.at[i], *dev_n).wait_recv()

        def go_next(i, s):
            return remote(buf.at[mine, i], buf.at[there_n, i], to_next.at[s], sems.at[i], *dev_n)

        def go_prev(i, s):
            return remote(buf.at[mine, i], buf.at[there_p, i], to_prev.at[s], sems.at[i], *dev_p)

        def when_next(even, act):
            if main:
                pl.when(jnp.logical_or(jnp.logical_not(near_extra), even))(act)
            else:
                act()

        def when_prev(odd, act):
            if main:
                pl.when(jnp.logical_or(jnp.logical_not(far_extra), odd))(act)
            else:
                act()

        def across(i):
            if main:

                @unless(extra)
                def _():
                    sibling(i).start()
            else:
                sibling(i).start()

        def own(n):
            i = here * NZ + away(n)
            arrive(i)
            when_next(n % 2 == 0, lambda: go_next(i, n).start())
            when_prev(n % 2 == 1, lambda: go_prev(i, n).start())
            across(i)

        def forward(j):
            i = before * NZ + away(2 * j)
            arrive(i)
            when_next(False, lambda: go_next(i, 8 + j).start())
            across(i)
            i = after * NZ + away(2 * j + 1)
            arrive(i)
            when_prev(False, lambda: go_prev(i, 8 + j).start())
            across(i)

        def rest(j):
            for i in (before * NZ + away(2 * j + 1), after * NZ + away(2 * j)):
                arrive(i)
                across(i)

        def far_side(n):
            i = opposite * NZ + away(n)
            arrive(i)
            across(i)

        def close(n):
            when_next(n % 2 == 0, lambda: go_next(n, n).wait_send())
            when_prev(n % 2 == 1, lambda: go_prev(n, n).wait_send())

        def close_forward(j):
            when_next(False, lambda: go_next(j, 8 + j).wait_send())
            when_prev(False, lambda: go_prev(j, 8 + j).wait_send())

        return own, forward, rest, far_side, close, close_forward

    main_ring, extra_ring = ring(True), ring(False)

    def send_queries():
        for h in range(HEADS):
            put(*q_args(h))

    def turns_of(step, length):
        def one(n, carry):
            if step == 0:
                pl.when(n == QUERIES_AT)(send_queries)
                pl.when(n + AHEAD < NZ)(lambda: issue(n + AHEAD))
            if step in (2, 3):
                unless(extra)(lambda: main_ring[step](n))
            else:
                main_ring[step](n)
            pl.when(extra)(lambda: extra_ring[step](n))
            return carry

        lax.fori_loop(0, length, one, 0)

    def from_sibling(quarter):
        def one(b, carry):
            i = quarter * NZ + b
            remote(buf.at[1 - c, i], buf.at[1 - c, i], ssib.at[i], rsib.at[i], p, sib).wait_recv()
            return carry

        lax.fori_loop(0, NZ, one, 0)

    ones = jnp.ones((16, KEYS), bf16)
    scale = math.log2(math.e) / math.sqrt(HD)

    def attend(quarter):
        ends = []
        total = 0
        for slot in range(SLOTS):
            total = total + jnp.clip((pairs[slot] + 1 - NZ * quarter + CHUNK - 1) // CHUNK, 0, PER_QUARTER)
            ends.append(total)

        def item(i):
            slot, base = 0, 0
            for s in range(SLOTS - 1):
                past = i >= ends[s]
                slot = slot + past.astype(jnp.int32)
                base = jnp.where(past, ends[s], base)
            return slot, quarter * PER_QUARTER + jnp.clip(i - base, 0, PER_QUARTER - 1), i < total

        def score(i, s):
            slot, chunk, _ = item(i)
            keys = buf[0, pl.ds(CHUNK * chunk, CHUNK)].reshape(KEYS, HD)
            s[...] = jnp.dot(keys, qbuf[slot], preferred_element_type=f32)

        def weigh(i, probs, keep):
            slot, chunk, _ = item(i)
            values = jnp.concatenate(
                [buf[1, CHUNK * chunk + b, g * TOK : (g + 1) * TOK, :] for b in range(CHUNK) for g in range(2)], axis=1
            )
            values = jnp.concatenate([values, ones], axis=0)
            acc[slot] = acc[slot] * keep[0:1] + jnp.dot(values, probs[...], preferred_element_type=f32)

        def soften(i, s, probs, keep):
            slot, chunk, valid = item(i)
            offset = bias[slot, chunk] + jnp.where(valid, 0.0, MASKED)
            old = row_max[slot, 0:1]
            new = old
            for g in range(PARTS):
                top = jnp.max(s[g * TOK : (g + 1) * TOK, :], axis=0, keepdims=True)
                new = jnp.maximum(new, top * scale + offset[g : g + 1])
            keep[...] = jnp.broadcast_to(jnp.exp2(old - new), (8, ROWS))
            row_max[slot] = jnp.broadcast_to(new, (8, ROWS))
            for g in range(PARTS):
                t = s[g * TOK : (g + 1) * TOK, :] * scale + (offset[g : g + 1] - new)
                probs[g * TOK : (g + 1) * TOK, :] = jnp.exp2(t).astype(bf16)

        score(0, s_a)
        p_b[...] = jnp.zeros_like(p_b)
        keep_b[...] = jnp.ones_like(keep_b)

        def two(n, carry):
            i = 2 * n
            weigh(jnp.maximum(i - 1, 0), p_b, keep_b)
            score(i + 1, s_b)
            soften(i, s_a, p_a, keep_a)
            weigh(i, p_a, keep_a)
            score(i + 2, s_a)
            soften(i + 1, s_b, p_b, keep_b)
            return carry

        turns = (total + 1) // 2
        lax.fori_loop(0, turns, two, 0)

        @pl.when(turns > 0)
        def _():
            weigh(2 * turns - 1, p_b, keep_b)

    pair_quarter = [pairs[slot] // NZ for slot in range(SLOTS)]

    def stage_of(quarter):
        stage = 0
        for n in range(1, 4):
            stage = jnp.where(order[n] == quarter, n, stage)
        return stage

    stages = [stage_of(quarter) for quarter in range(4)]
    upto = [stages[0]]
    for quarter in range(1, 4):
        upto.append(jnp.maximum(upto[-1], stages[quarter]))

    def pick_one(values, i):
        chosen = values[0]
        for n in range(1, len(values)):
            chosen = jnp.where(i == n, values[n], chosen)
        return chosen

    def o_args(slot, g):
        pd = pick_one(pairs, slot) - 1 + g
        dst = att.at[pl.ds((1 - g) * TOK, TOK), pl.ds(pl.multiple_of(head * HD, HD), HD)]
        return o_buf.at[slot, g], dst, osend.at[2 * slot + g], orecv.at[(1 - g) * HEADS + head], pd, home

    def mix(slot, g):
        cols = slice(g * TOK, (g + 1) * TOK)
        o_buf[slot, g] = (acc[slot, :HD, cols] / acc[slot, HD : HD + 1, cols]).T.astype(bf16)

    def finish(stage):
        def one(slot, carry):
            pair = pick_one(pairs, slot)

            @pl.when(jnp.logical_and(pair >= 0, pick_one(upto, pair // NZ) == stage))
            def _():
                mix(slot, 1)
                put(*o_args(slot, 1))

            return carry

        lax.fori_loop(0, SLOTS, one, 0)

    turns_of(0, NZ)
    turns_of(1, 4)
    from_sibling(order[0])
    for slot in range(SLOTS):

        @pl.when(pairs[slot] >= 0)
        def _():
            remote(qt.at[0], qbuf.at[slot], qsend.at[0], qrecv.at[slot], p, hd).wait_recv()

    attend(order[0])
    finish(0)
    turns_of(2, 4)
    from_sibling(order[1])
    attend(order[1])
    finish(1)
    from_sibling(order[2])
    turns_of(3, NZ)
    attend(order[2])
    finish(2)
    from_sibling(order[3])
    attend(order[3])
    finish(3)

    def second_half(slot, carry):
        @pl.when(pick_one(pairs, slot) >= 0)
        def _():
            mix(slot, 0)
            put_done(*o_args(slot, 1))

        @pl.when(pick_one(pairs, slot) >= 1)
        def _():
            put(*o_args(slot, 0))

        return carry

    lax.fori_loop(0, SLOTS, second_half, 0)

    def o_arrive(g):
        for h in range(HEADS):
            dst = att.at[pl.ds(g * TOK, TOK), pl.ds(h * HD, HD)]
            remote(dst, dst, osend.at[0], orecv.at[g * HEADS + h], p, hd).wait_recv()

    turn = (xo, xn, xp, x)

    def half_rows(t):
        return slice(t * TOK, (t + 1) * TOK)

    def part(t, j, core):
        cols = pl.ds(pl.multiple_of((2 * turn[j] + core) * WIDTH, HD), WIDTH)
        return jnp.dot(att[half_rows(t), :], w[:, cols], preferred_element_type=f32)

    def over(t, j):
        return remote(s1.at[t, j], r1.at[t, j], send1.at[4 * t + j], recv1.at[4 * t + j], p, sib)

    piece = TOK // PIECES

    def piece_rows(u):
        return slice(u * piece, (u + 1) * piece)

    def far_copy(t, u):
        i = PIECES * t + u
        rows = pl.ds(u * piece, piece)
        return remote(far.at[t, rows], far_in.at[t, rows], fsend.at[i], frecv.at[i], p, 2 * (xn, xp)[t] + c)

    def near_copy(t, d, u):
        i = PIECES * (2 * t + d) + u
        rows = pl.ds(u * piece, piece)
        return remote(near.at[t, d, rows], near_in.at[t, d, rows], nsend.at[i], nrecv.at[i], p, 2 * (xn, xp)[d] + c)

    def send_parts(t):
        through, direct = t, 1 - t

        def for_sibling(j):
            s1[t, j] = part(t, j, 1 - c).astype(bf16)
            over(t, j).start()

        def both(j, mine):
            over(t, j).wait_recv()
            return mine + r1[t, j].astype(f32)

        for_sibling(0)
        for_sibling(1 + direct)
        far[t] = both(0, part(t, 0, c)).astype(bf16)
        for u in range(PIECES):
            far_copy(t, u).start()
        near[t, direct] = both(1 + direct, part(t, 1 + direct, c)).astype(bf16)
        for u in range(PIECES):
            near_copy(t, direct, u).start()
        for_sibling(1 + through)
        for_sibling(3)
        through_sum = both(1 + through, part(t, 1 + through, c))
        for u in range(PIECES):
            rows = piece_rows(u)
            far_copy(t, u).wait_recv()
            near[t, through, rows] = (through_sum[rows] + far_in[t, rows].astype(f32)).astype(bf16)
            near_copy(t, through, u).start()
        keep[half_rows(t), :] = both(3, part(t, 3, c))

    def all_parts(t):
        total = keep[half_rows(t), :]
        for d in (1 - t, t):
            for u in range(PIECES):
                near_copy(t, d, u).wait_recv()
            total = total + near_in[t, d].astype(f32)
        return total

    loads[6].wait()
    loads[7].wait()
    o_arrive(0)
    send_parts(0)

    @unless(last)
    def _():
        o_arrive(1)

    send_parts(1)
    out_ref[:TOK, :] = (hid[TOK:, :].astype(f32) + gate[pl.ds(levels[1], 1), :] * all_parts(0)).astype(bf16)
    summed = all_parts(1)

    @pl.when(last)
    def _():
        out_ref[TOK:, :] = inc[...]

    @unless(last)
    def _():
        for copy in shift:
            copy.wait_recv()
        out_ref[TOK:, :] = (hs[...].astype(f32) + gs[0:1, :] * summed).astype(bf16)

    @pl.when(p > 0)
    def _():
        for copy in shift:
            copy.wait_send()

    for h in range(HEADS):
        for k in range(2):
            put_done(*(main_args(h, k) if h < 4 else extra_args(k)))
        put_done(*q_args(h))
    turns_of(4, NZ)
    turns_of(5, 4)

    def sibling_done(i, carry):
        sibling(i).wait_send()
        return carry

    lax.fori_loop(0, PAIRS, sibling_done, 0)
    for slot in range(SLOTS):

        @pl.when(pairs[slot] >= 1)
        def _():
            put_done(*o_args(slot, 0))

    for t in range(2):
        for j in range(4):
            over(t, j).wait_send()
        for u in range(PIECES):
            far_copy(t, u).wait_send()
            for d in range(2):
                near_copy(t, d, u).wait_send()


def on_device(query_states, key_states, value_states, hidden, out_weight, gate_table, levels, visible, incoming):
    dma = pltpu.SemaphoreType.DMA
    vmem = pltpu.VMEM
    return pl.pallas_call(
        body,
        out_shape=jax.ShapeDtypeStruct((ROWS, WIDTH), bf16),
        in_specs=[ANY] * 6 + [pl.BlockSpec(memory_space=pltpu.SMEM)] + [ANY] * 2,
        out_specs=pl.BlockSpec(memory_space=pltpu.VMEM),
        scratch_shapes=[
            vmem((ROWS, WIDTH), bf16),
            vmem((ROWS, WIDTH), bf16),
            vmem((ROWS, WIDTH), bf16),
            vmem((ROWS, WIDTH), bf16),
            vmem((WIDTH, 8 * WIDTH), bf16),
            vmem((LEVELS, WIDTH), f32),
            vmem((64, 64), jnp.int32),
            vmem((TOK, WIDTH), bf16),
            vmem((3, PAIRS, ROWS, HD), bf16),
            vmem((SLOTS, HD, ROWS), bf16),
            vmem((HEADS, HD, ROWS), bf16),
            vmem((HEADS, ROWS, HD), bf16),
            vmem((SLOTS, PAIRS // CHUNK, PARTS, ROWS), f32),
            vmem((KEYS, ROWS), f32),
            vmem((KEYS, ROWS), f32),
            vmem((KEYS, ROWS), bf16),
            vmem((KEYS, ROWS), bf16),
            vmem((8, ROWS), f32),
            vmem((8, ROWS), f32),
            vmem((SLOTS, 8, ROWS), f32),
            vmem((SLOTS, HD + 16, ROWS), f32),
            vmem((SLOTS, 2, TOK, HD), bf16),
            vmem((ROWS, WIDTH), bf16),
            vmem((2, 4, TOK, WIDTH), bf16),
            vmem((2, 4, TOK, WIDTH), bf16),
            vmem((2, TOK, WIDTH), bf16),
            vmem((2, TOK, WIDTH), bf16),
            vmem((2, 2, TOK, WIDTH), bf16),
            vmem((2, 2, TOK, WIDTH), bf16),
            vmem((ROWS, WIDTH), f32),
            vmem((TOK, WIDTH), bf16),
            vmem((8, WIDTH), f32),
            vmem((8, WIDTH), f32),
            dma((8,)),
            dma((5,)),
            dma((5,)),
            dma((5,)),
            dma((SLOTS,)),
            dma((PAIRS,)),
            dma((PAIRS,)),
            dma((PAIRS,)),
            dma((12,)),
            dma((12,)),
            dma((12,)),
            dma((12,)),
            dma((PAIRS,)),
            dma((2 * SLOTS,)),
            dma((2 * HEADS,)),
            dma((8,)),
            dma((8,)),
            dma((2 * PIECES,)),
            dma((2 * PIECES,)),
            dma((4 * PIECES,)),
            dma((4 * PIECES,)),
            dma((2,)),
            dma((2,)),
        ],
        compiler_params=pltpu.CompilerParams(has_side_effects=True, collective_id=0, vmem_limit_bytes=56 << 20),
        name="block",
    )(query_states, key_states, value_states, hidden, out_weight, gate_table, levels, visible, incoming)


def solution(mesh):
    return jax.shard_map(
        on_device,
        mesh=mesh,
        in_specs=(
            P("group", "head"),
            P("group", "head"),
            P("group", "head"),
            P("group", "head"),
            P("head", None),
            P(None, "head"),
            P("group"),
            P(),
            P(None, "head"),
        ),
        out_specs=P("group", "head"),
        check_vma=False,
    )
```
